32 devices in a mesh: px: 4 (over z), py: 8 (over y, x, core).
Axes of the slice: x: 2, y: 2, z: 4, core: 2. Of those that a mesh axis runs over, the one named last changes fastest.
Arguments:
- coupling: bfloat16 [4, 8, 64, 218, 125], P('px', 'py'), may hold values from -0.5 to 0.5
- interior_inverse: bfloat16 [4, 8, 64, 125, 125], P('px', 'py'), may hold values from -0.5 to 0.5
- interior_load: bfloat16 [4, 8, 64, 125, 256], P('px', 'py'), may hold values from -6 to 6
- boundary_load: bfloat16 [4, 8, 4608, 256], P('px', 'py'), may hold values from -6 to 6
- owner_weight: float32 [4, 8, 4608], P('px', 'py'), may hold values from 0.5 to 4
- elem_weight: float32 [4, 8, 64, 218], P('px', 'py'), may hold values from 0.25 to 1
- elem_dof: int32 [4, 8, 64, 218], P('px', 'py'), may hold values from 0 to 5999, as said below
- reader_rows: int32 [4, 8, 4, 348], P('px', 'py'), may hold values from 0 to 4607, as said below
- elem_count: int32 [4, 8], P('px', 'py'), may hold values from 16 to 64, as said below
Outputs:
- face_values: float32 [4, 8, 4608, 256], P('px', 'py')
- interior_values: bfloat16 [4, 8, 64, 125, 256], P('px', 'py')
The draws below stay inside these ranges and needn't reach their ends.
Inputs may be any that keep to these rules, and one draw needn't show every extreme that they name: `elem_dof`: rows below 4608 are the partition's own boundary rows; row 4608 + k * 348 + s is the s-th row that the partition shares with its neighbour in direction k. The modes of slot e name only rows r with r % 8 equal to e // 8. Every local row is named by at least two of the partition's modes. `reader_rows`: entry [k, s] is the owned row that the neighbour in direction k refers to by its row 4608 + opp(k) * 348 + s; the 1392 entries of one partition are distinct. `elem_count`: slots at or past a partition's count are empty.
All inputs are finite; a program needn't handle non-finite values.
Results may differ from the reference program's by a relative error of at most 0.0056.
Values may be sent and summed in bfloat16 or wider, within the bound.
A program may use at most 128 MiB of HBM per device.

```python
import math
import jax
import jax.numpy as jnp
from jax import lax

NB = 218
NI = 125
R = 256
E_DEV = 64
GS = 8
NG = 8
OWN = 4608
SH = 348
LOC = 6000
GX = 4
GY = 8


def draw_elem_dof(key, part):
    keys = jax.random.split(key, GX * GY)
    entries = GS * NB

    def one_partition(sub_key):
        blocks = []
        for group_index in range(NG):
            group_key = jax.random.fold_in(sub_key, group_index)
            first_key, second_key = jax.random.split(group_key)
            row_count = (LOC - group_index + NG - 1) // NG
            base_rows = group_index + NG * jnp.arange(row_count, dtype=jnp.int32)
            spare = entries - 2 * row_count
            extra_rows = group_index + NG * jax.random.randint(first_key, (spare,), 0, row_count).astype(jnp.int32)
            listed = jnp.concatenate([base_rows, base_rows, extra_rows])
            mixed = jax.random.permutation(second_key, listed)
            blocks.append(mixed.astype(jnp.int32).reshape(GS, NB))
        return jnp.concatenate(blocks, axis=0)
    return jax.vmap(one_partition)(keys).reshape(GX, GY, E_DEV, NB)


def draw_reader_rows(key, part):
    keys = jax.random.split(key, GX * GY)

    def one_partition(sub_key):
        first_key, second_key = jax.random.split(sub_key)
        scores = jax.random.permutation(first_key, OWN).astype(jnp.int32)
        scores = scores.at[0].set(-2).at[OWN - 1].set(-1)
        ordered = jnp.argsort(scores, stable=True)[:4 * SH]
        mixing = jax.random.permutation(second_key, 4 * SH)
        return ordered[mixing].astype(jnp.int32)
    return jax.vmap(one_partition)(keys).reshape(GX, GY, 4, SH)


def draw_elem_count(key, part):
    first_key, second_key, third_key = jax.random.split(key, 3)
    total_parts = GX * GY
    counts = jax.random.randint(first_key, (total_parts,), E_DEV // 4, E_DEV + 1)
    fullest = jax.random.randint(second_key, (), 0, total_parts)
    emptiest = (fullest + 1 + jax.random.randint(third_key, (), 0, total_parts - 1)) % total_parts
    counts = counts.at[fullest].set(E_DEV).at[emptiest].set(E_DEV // 4)
    return counts.reshape(GX, GY).astype(jnp.int32)


def shard_levels(key, extent, shards, least, high):
    loudness, own = 1.0, jax.random.fold_in(key, 6)
    for axis_at, blocks in shards:
        draws = jnp.exp(jax.random.uniform(jax.random.fold_in(own, axis_at), (blocks,), jnp.float32, least / len(shards), high / len(shards)))
        loudness = loudness * jnp.repeat(draws, extent[axis_at] // blocks).reshape([-1 if axis == axis_at else 1 for axis in range(len(extent))])
    return loudness


def bell_draw(own_key, shape, spread, limit, cuts=(), kind=jnp.bfloat16):
    values = spread * jax.random.normal(own_key, shape, jnp.float32)
    if cuts:
        values = values * shard_levels(own_key, shape, cuts, -0.22, 0.18)
    return jnp.clip(values, -limit, limit).astype(kind)


def setup_inputs(seed: int = 0) -> dict:
    arg_keys = jax.random.split(jax.random.key(seed), 10)
    coupling = bell_draw(arg_keys[0], (GX, GY, E_DEV, NB, NI), NI ** -0.5, 0.5, ((0, 4), (1, 8)))
    interior_inverse = bell_draw(arg_keys[1], (GX, GY, E_DEV, NI, NI), NI ** -0.5, 0.5, ((0, 4), (1, 8)))
    interior_load = bell_draw(arg_keys[2], (GX, GY, E_DEV, NI, R), 1.0, 6.0, ((0, 4), (1, 8)))
    boundary_load = bell_draw(arg_keys[3], (GX, GY, OWN, R), 1.0, 6.0, ((0, 4), (1, 8)))
    owner_weight = jnp.clip(jnp.exp(math.log(4.0) - 2.0794415 * jax.random.uniform(arg_keys[4], (GX, GY, OWN), jnp.float32) ** shard_levels(arg_keys[4], (GX, GY, OWN), ((0, 4), (1, 8)), -0.2, 0.2)), 0.5, 4.0)
    elem_weight = jnp.clip(jnp.exp(math.log(1.0) - 1.3862944 * jax.random.uniform(arg_keys[5], (GX, GY, E_DEV, NB), jnp.float32) ** shard_levels(arg_keys[5], (GX, GY, E_DEV, NB), ((0, 4), (1, 8)), -0.2, 0.2)), 0.25, 1.0)
    elem_dof = draw_elem_dof(jax.random.fold_in(arg_keys[9], 71), 0)
    reader_rows = draw_reader_rows(jax.random.fold_in(arg_keys[9], 71), 0)
    elem_count = draw_elem_count(jax.random.fold_in(arg_keys[9], 71), 0)
    return dict(coupling=coupling, interior_inverse=interior_inverse, interior_load=interior_load, boundary_load=boundary_load, owner_weight=owner_weight, elem_weight=elem_weight, elem_dof=elem_dof, reader_rows=reader_rows, elem_count=elem_count)


step_table = ((-1, 0), (1, 0), (0, -1), (0, 1))
opposite_table = (1, 0, 3, 2)


def condense_part(items):
    coupling, inverse, interior_rhs, slot_weight, dof_rows, live_count = items
    live_slots = jnp.arange(E_DEV) < live_count
    solved = jnp.einsum("eij,ejr->eir", inverse.astype(jnp.float32), interior_rhs.astype(jnp.float32)).astype(jnp.bfloat16)
    solved = lax.optimization_barrier(solved)
    slot_terms = jnp.einsum("ebi,eir->ebr", coupling.astype(jnp.float32), solved.astype(jnp.float32))
    slot_terms = jnp.where(live_slots[:, None, None], slot_terms, 0.0)
    live_weight = jnp.where(live_slots[:, None], slot_weight, 0.0)
    flat_rows = dof_rows.reshape(-1)
    local_rows = jnp.zeros((LOC, R), jnp.float32).at[flat_rows].add(slot_terms.reshape(-1, R))
    local_weight = jnp.zeros((LOC,), jnp.float32).at[flat_rows].add(live_weight.reshape(-1))
    return local_rows, local_weight


def recover_part(items):
    coupling, inverse, interior_rhs, local_values, dof_rows, live_count = items
    live_slots = jnp.arange(E_DEV) < live_count
    boundary = jnp.take(local_values, dof_rows.reshape(-1), axis=0).reshape(E_DEV, NB, R)
    pulled = jnp.einsum("ebi,ebr->eir", coupling.astype(jnp.float32), boundary.astype(jnp.float32))
    reduced = (interior_rhs.astype(jnp.float32) - pulled).astype(jnp.bfloat16)
    reduced = lax.optimization_barrier(reduced)
    result = jnp.einsum("eij,ejr->eir", inverse.astype(jnp.float32), reduced.astype(jnp.float32))
    return jnp.where(live_slots[:, None, None], result, 0.0).astype(jnp.bfloat16)


def neighbour_of(array_in, direction):
    step_x, step_y = step_table[direction]
    return jnp.roll(array_in, (-step_x, -step_y), axis=(0, 1))


def scatter_owned(readers, values_in):
    tail_shape = values_in.shape[2:]
    return jnp.zeros((OWN,) + tail_shape, jnp.float32).at[readers.reshape(-1)].add(values_in.reshape((-1,) + tail_shape))


def pick_rows(face_part, readers):
    return face_part[readers.reshape(-1)].reshape(4, SH, R)


def reference(coupling, interior_inverse, interior_load, boundary_load, owner_weight, elem_weight, elem_dof, reader_rows, elem_count):
    parts = GX * GY

    def flatten(array_in):
        return array_in.reshape((parts,) + array_in.shape[2:])

    local_rows, local_weight = lax.map(condense_part, (flatten(coupling), flatten(interior_inverse), flatten(interior_load), flatten(elem_weight), flatten(elem_dof), flatten(elem_count)))
    local_rows = local_rows.reshape(GX, GY, LOC, R)
    local_weight = local_weight.reshape(GX, GY, LOC)
    pre_total = boundary_load.astype(jnp.float32) - local_rows[:, :, :OWN]
    pre_weight = owner_weight + local_weight[:, :, :OWN]
    shared_rows = local_rows[:, :, OWN:].reshape(GX, GY, 4, SH, R)
    shared_weight = local_weight[:, :, OWN:].reshape(GX, GY, 4, SH)
    incoming = jnp.stack([neighbour_of(shared_rows[:, :, opposite_table[direction]], direction) for direction in range(4)], axis=2)
    incoming_weight = jnp.stack([neighbour_of(shared_weight[:, :, opposite_table[direction]], direction) for direction in range(4)], axis=2)
    flat_readers = reader_rows.reshape(parts, 4, SH)
    added = jax.vmap(scatter_owned)(flat_readers, incoming.reshape(parts, 4, SH, R)).reshape(GX, GY, OWN, R)
    added_weight = jax.vmap(scatter_owned)(flat_readers, incoming_weight.reshape(parts, 4, SH)).reshape(GX, GY, OWN)
    face_values = (pre_total - added) / (pre_weight + added_weight)[..., None]
    gathered = jax.vmap(pick_rows)(face_values.reshape(parts, OWN, R), flat_readers).reshape(GX, GY, 4, SH, R)
    returned = jnp.stack([neighbour_of(gathered[:, :, opposite_table[direction]], direction) for direction in range(4)], axis=2)
    local_values = jnp.concatenate([face_values, returned.reshape(GX, GY, 4 * SH, R)], axis=2).astype(jnp.bfloat16)
    interior_values = lax.map(recover_part, (flatten(coupling), flatten(interior_inverse), flatten(interior_load), local_values.reshape(parts, LOC, R), flatten(elem_dof), flatten(elem_count)))
    return face_values, interior_values.reshape(GX, GY, E_DEV, NI, R)
```

```python
import functools

import jax
import jax.numpy as jnp
from jax import lax
from jax.experimental import pallas as pl
from jax.experimental.pallas import tpu as pltpu
from jax.sharding import PartitionSpec as P

GS = 8
LANES = 128
VMEM_BYTES = 58 * 2**20
OPPOSITE = (1, 0, 3, 2)


def round_up(value, unit):
    return (value + unit - 1) // unit * unit


def condense_kernel(
    sizes,
    count_ref,
    readers_ref,
    inverse_ref,
    load_ref,
    coupling_ref,
    weight_ref,
    dof_ref,
    edge_ref,
    owner_ref,
    spread_ref,
    pre_ref,
    pre_weight_ref,
    mine_ref,
    mine_weight_ref,
    picked_ref,
    picked_weight_ref,
    pay_ref,
    pay_weight_ref,
    local_ref,
    local_weight_ref,
    solved_ref,
    coupling_ext_ref,
):
    slots, modes, inner, columns, owned, shared, windows, pad_shared = sizes
    group = pl.program_id(0)
    halves = columns // LANES

    @pl.when(group == 0)
    def _():
        solved_ref[...] = jnp.zeros_like(solved_ref)
        coupling_ext_ref[...] = jnp.zeros_like(coupling_ext_ref)
        picked_ref[...] = jnp.zeros_like(picked_ref)
        picked_weight_ref[...] = jnp.ones_like(picked_weight_ref)
        mine_ref[...] = jnp.zeros_like(mine_ref)
        mine_weight_ref[...] = jnp.ones_like(mine_weight_ref)

    count = count_ref[0, 0]
    lane = lax.broadcasted_iota(jnp.int32, (modes, LANES), 1)
    window_ids = lax.broadcasted_iota(jnp.int32, (windows, modes), 0)
    weight_cols = weight_ref[...].T
    window_of = dof_ref[...] // GS
    weight_total = jnp.zeros((windows, LANES), jnp.float32)
    for e in range(GS):
        live = group * GS + e < count
        solved = jnp.dot(inverse_ref[e], load_ref[e], preferred_element_type=jnp.float32)
        solved = jnp.where(live, solved, 0.0).astype(jnp.bfloat16)
        solved_ref[e, :inner, :] = solved
        coupling_ext_ref[:modes, :inner] = coupling_ref[e]
        col = jnp.where(live, weight_cols[:, e : e + 1], 0.0)
        high = col.astype(jnp.bfloat16).astype(jnp.float32)
        mid = (col - high).astype(jnp.bfloat16).astype(jnp.float32)
        low = col - high - mid
        extra = jnp.where(lane == inner, high, jnp.where(lane == inner + 1, mid, low))
        ext = jnp.where(
            lane < inner, coupling_ext_ref[:modes, :].astype(jnp.float32), extra
        ).astype(jnp.bfloat16)
        onehot = (window_ids == window_of[e : e + 1, :]).astype(jnp.bfloat16)
        spread = jnp.dot(onehot, ext, preferred_element_type=jnp.float32)
        weight_total = weight_total + spread
        spread_ref[:, e * LANES : (e + 1) * LANES] = spread.astype(jnp.bfloat16)

    rows = jnp.dot(
        spread_ref[...],
        solved_ref[...].reshape(GS * LANES, columns),
        preferred_element_type=jnp.float32,
    )
    wide_lane = lax.broadcasted_iota(jnp.int32, (windows, LANES), 1)
    weight_sum = jnp.sum(jnp.where(wide_lane >= inner, weight_total, 0.0), axis=1, keepdims=True)
    for c in range(halves):
        local_ref[c, pl.ds(group, windows, stride=GS), :] = rows[:, c * LANES : (c + 1) * LANES]
    local_weight_ref[pl.ds(group, windows, stride=GS), :] = jnp.broadcast_to(
        weight_sum, (windows, LANES)
    )

    @pl.when(group == pl.num_programs(0) - 1)
    def _():
        def subtract(chunk, carry):
            at = pl.ds(pl.multiple_of(chunk * LANES, LANES), LANES)
            for c in range(halves):
                pre_ref[c, at, :] = (
                    edge_ref[at, c * LANES : (c + 1) * LANES].astype(jnp.float32)
                    - local_ref[c, at, :]
                )
            own = jnp.broadcast_to(owner_ref[pl.ds(chunk, 1), :], (LANES, LANES)).T
            pre_weight_ref[at, :] = own + local_weight_ref[at, :]
            return carry

        lax.fori_loop(0, owned // LANES, subtract, 0)

        def pick(s, carry):
            loaded = []
            for k in range(4):
                r = readers_ref[k, s]
                loaded.append(
                    (
                        [pre_ref[c, pl.ds(r, 1), :] for c in range(halves)],
                        pre_weight_ref[pl.ds(r, 1), :],
                    )
                )
            for k in range(4):
                values, weight = loaded[k]
                for c in range(halves):
                    picked_ref[k, c, pl.ds(s, 1), :] = values[c]
                picked_weight_ref[k, pl.ds(s, 1), :] = weight
            return carry

        lax.fori_loop(0, shared, pick, 0, unroll=4)
        for k in range(4):
            start = owned + k * shared
            for c in range(halves):
                cols = slice(c * LANES, (c + 1) * LANES)
                mine = local_ref[c, start : start + shared, :]
                mine_ref[k, c, :shared, :] = mine
                pay_ref[k, 0, :, cols] = mine_ref[k, c].astype(jnp.bfloat16)
                pay_ref[k, 1, :, cols] = picked_ref[k, c].astype(jnp.bfloat16)
            mine_weight_ref[k, :shared, :] = local_weight_ref[start : start + shared, :]
            sub = lax.broadcasted_iota(jnp.int32, (8, pad_shared), 0)
            pay_weight_ref[k] = jnp.where(
                sub == 0, mine_weight_ref[k].T[:8], picked_weight_ref[k].T[:8]
            )


def exchange_kernel(counts, pay_ref, weight_ref, got_ref, got_weight_ref, send_sem, recv_sem):
    nx, ny = counts
    a, b = lax.axis_index("px"), lax.axis_index("py")
    targets = (
        (lax.rem(a + nx - 1, nx), b),
        (lax.rem(a + 1, nx), b),
        (a, lax.rem(b + ny - 1, ny)),
        (a, lax.rem(b + 1, ny)),
    )
    barrier = pltpu.get_barrier_semaphore()
    for target in targets:
        pl.semaphore_signal(
            barrier, inc=1, device_id=target, device_id_type=pl.DeviceIdType.MESH
        )
    pl.semaphore_wait(barrier, 4)
    copies = []
    for k in range(4):
        for part, (source, dest) in enumerate(((pay_ref, got_ref), (weight_ref, got_weight_ref))):
            copy = pltpu.make_async_remote_copy(
                src_ref=source.at[k],
                dst_ref=dest.at[OPPOSITE[k]],
                send_sem=send_sem.at[part, k],
                recv_sem=recv_sem.at[part, OPPOSITE[k]],
                device_id=targets[k],
                device_id_type=pl.DeviceIdType.MESH,
            )
            copy.start()
            copies.append(copy)
    for copy in copies:
        copy.wait()


def recover_kernel(
    sizes,
    count_ref,
    readers_ref,
    got_ref,
    got_weight_ref,
    pre_ref,
    pre_weight_ref,
    mine_ref,
    mine_weight_ref,
    picked_ref,
    picked_weight_ref,
    spread_ref,
    inverse_ref,
    load_ref,
    face_ref,
    out_ref,
    values_ref,
    ready_ref,
):
    slots, modes, inner, columns, owned, shared, windows, pad_shared = sizes
    group = pl.program_id(0)
    halves = columns // LANES
    groups = slots // GS
    part = owned // groups

    @pl.when(group == 0)
    def _():
        def divide(chunk, carry):
            at = pl.ds(pl.multiple_of(chunk * LANES, LANES), LANES)
            scale = 1.0 / pre_weight_ref[at, :]
            for c in range(halves):
                values_ref[c, at, :] = pre_ref[c, at, :] * scale
            return carry

        lax.fori_loop(0, owned // LANES, divide, 0)
        tail = owned + 4 * shared
        for k in range(4):
            weights = got_weight_ref[k].T
            to_mine = 1.0 / (picked_weight_ref[k] + weights[:, 0:1])
            to_theirs = 1.0 / (mine_weight_ref[k] + weights[:, 1:2])
            start = owned + k * shared
            for c in range(halves):
                cols = slice(c * LANES, (c + 1) * LANES)
                ready_ref[k, c] = (
                    picked_ref[k, c] - got_ref[k, 0, :, cols].astype(jnp.float32)
                ) * to_mine
                theirs = (
                    got_ref[k, 1, :, cols].astype(jnp.float32) - mine_ref[k, c]
                ) * to_theirs
                values_ref[c, start : start + shared, :] = theirs[:shared]
        if windows * GS > tail:
            for c in range(halves):
                values_ref[c, tail:, :] = jnp.zeros((windows * GS - tail, LANES), jnp.float32)

        def place(s, carry):
            loaded = []
            for k in range(4):
                loaded.append([ready_ref[k, c, pl.ds(s, 1), :] for c in range(halves)])
            for k in range(4):
                r = readers_ref[k, s]
                for c in range(halves):
                    values_ref[c, pl.ds(r, 1), :] = loaded[k][c]
            return carry

        lax.fori_loop(0, shared, place, 0, unroll=4)

    at = pl.ds(pl.multiple_of(group * part, 8), part)
    for c in range(halves):
        face_ref[:, c * LANES : (c + 1) * LANES] = values_ref[c, at, :]

    table = jnp.concatenate(
        [values_ref[c, pl.ds(group, windows, stride=GS), :] for c in range(halves)], axis=1
    )
    turned = table.T.astype(jnp.bfloat16)
    pulled_turned = jnp.dot(turned, spread_ref[...], preferred_element_type=jnp.float32)
    count = count_ref[0, 0]
    for e in range(GS):
        live = group * GS + e < count
        pulled = pulled_turned[:, e * LANES : (e + 1) * LANES].T[:inner]
        reduced = (load_ref[e].astype(jnp.float32) - pulled).astype(jnp.bfloat16)
        result = jnp.dot(inverse_ref[e], reduced, preferred_element_type=jnp.float32)
        out_ref[e] = jnp.where(live, result, 0.0).astype(jnp.bfloat16)


def per_device(
    counts,
    coupling,
    interior_inverse,
    interior_load,
    boundary_load,
    owner_weight,
    elem_weight,
    elem_dof,
    reader_rows,
    elem_count,
):
    slots, modes, inner = coupling.shape[2:]
    columns = interior_load.shape[-1]
    owned = boundary_load.shape[2]
    shared = reader_rows.shape[3]
    groups = slots // GS
    halves = columns // LANES
    windows = round_up((owned + 4 * shared) // GS, 16)
    pad_shared = round_up(shared, LANES)
    sizes = (slots, modes, inner, columns, owned, shared, windows, pad_shared)
    f32, bf16 = jnp.float32, jnp.bfloat16
    smem = pl.BlockSpec(memory_space=pltpu.SMEM)
    vmem = pl.BlockSpec(memory_space=pltpu.VMEM)
    anyplace = pl.BlockSpec(memory_space=pl.ANY)

    def by_group(*tail):
        zeros = (0,) * (len(tail))
        return pl.BlockSpec((None, None, GS) + tail, lambda g: (0, 0, g) + zeros)

    spread_spec = pl.BlockSpec((None, windows, GS * LANES), lambda g: (g, 0, 0))
    readers = reader_rows[0, 0]
    params = dict(vmem_limit_bytes=VMEM_BYTES, dimension_semantics=("arbitrary",))
    shape = jax.ShapeDtypeStruct
    (
        spread,
        pre,
        pre_weight,
        mine,
        mine_weight,
        picked,
        picked_weight,
        pay,
        pay_weight,
    ) = pl.pallas_call(
        functools.partial(condense_kernel, sizes),
        grid=(groups,),
        in_specs=[
            smem,
            smem,
            by_group(inner, inner),
            by_group(inner, columns),
            by_group(modes, inner),
            by_group(modes),
            by_group(modes),
            vmem,
            vmem,
        ],
        out_specs=[spread_spec] + [vmem] * 8,
        out_shape=[
            shape((groups, windows, GS * LANES), bf16),
            shape((halves, owned, LANES), f32),
            shape((owned, LANES), f32),
            shape((4, halves, pad_shared, LANES), f32),
            shape((4, pad_shared, LANES), f32),
            shape((4, halves, pad_shared, LANES), f32),
            shape((4, pad_shared, LANES), f32),
            shape((4, 2, pad_shared, columns), bf16),
            shape((4, 8, pad_shared), f32),
        ],
        scratch_shapes=[
            pltpu.VMEM((halves, windows * GS, LANES), f32),
            pltpu.VMEM((windows * GS, LANES), f32),
            pltpu.VMEM((GS, LANES, columns), bf16),
            pltpu.VMEM((round_up(modes, 16), LANES), bf16),
        ],
        compiler_params=pltpu.CompilerParams(**params),
        name="condense",
    )(
        elem_count,
        readers,
        interior_inverse,
        interior_load,
        coupling,
        elem_weight,
        elem_dof,
        boundary_load[0, 0],
        owner_weight.reshape(owned // LANES, LANES),
    )
    got, got_weight = pl.pallas_call(
        functools.partial(exchange_kernel, counts),
        in_specs=[anyplace, anyplace],
        out_specs=[anyplace, anyplace],
        out_shape=[shape(pay.shape, bf16), shape(pay_weight.shape, f32)],
        scratch_shapes=[pltpu.SemaphoreType.DMA((2, 4)), pltpu.SemaphoreType.DMA((2, 4))],
        compiler_params=pltpu.CompilerParams(collective_id=0, has_side_effects=True),
        name="exchange",
    )(pay, pay_weight)
    face, interior = pl.pallas_call(
        functools.partial(recover_kernel, sizes),
        grid=(groups,),
        in_specs=[smem, smem]
        + [vmem] * 8
        + [spread_spec, by_group(inner, inner), by_group(inner, columns)],
        out_specs=[
            pl.BlockSpec((None, None, owned // groups, columns), lambda g: (0, 0, g, 0)),
            by_group(inner, columns),
        ],
        out_shape=[
            shape((1, 1, owned, columns), f32),
            shape((1, 1, slots, inner, columns), bf16),
        ],
        scratch_shapes=[
            pltpu.VMEM((halves, windows * GS, LANES), f32),
            pltpu.VMEM((4, halves, pad_shared, LANES), f32),
        ],
        compiler_params=pltpu.CompilerParams(**params),
        name="recover",
    )(
        elem_count,
        readers,
        got,
        got_weight,
        pre,
        pre_weight,
        mine,
        mine_weight,
        picked,
        picked_weight,
        spread,
        interior_inverse,
        interior_load,
    )
    return face, interior


def solution(mesh):
    in_specs = (
        P("px", "py", None, None, None),
        P("px", "py", None, None, None),
        P("px", "py", None, None, None),
        P("px", "py", None, None),
        P("px", "py", None),
        P("px", "py", None, None),
        P("px", "py", None, None),
        P("px", "py", None, None),
        P("px", "py"),
    )
    out_specs = (P("px", "py", None, None), P("px", "py", None, None, None))
    counts = (mesh.shape["px"], mesh.shape["py"])
    return jax.shard_map(
        functools.partial(per_device, counts),
        mesh=mesh,
        in_specs=in_specs,
        out_specs=out_specs,
        check_vma=False,
    )
```

```python
import functools

import jax
import jax.numpy as jnp
from jax import lax
from jax.experimental import pallas as pl
from jax.experimental.pallas import tpu as pltpu
from jax.sharding import PartitionSpec as P

GS = 8
LANES = 128
VMEM_BYTES = 58 * 2**20
OPPOSITE = (1, 0, 3, 2)


def round_up(value, unit):
    return (value + unit - 1) // unit * unit


def condense_kernel(
    sizes,
    counts,
    count_ref,
    readers_ref,
    inverse_ref,
    load_ref,
    coupling_ref,
    weight_ref,
    dof_ref,
    edge_ref,
    owner_ref,
    spread_ref,
    inverse_out_ref,
    load_out_ref,
    values_ref,
    ready_ref,
    local_ref,
    local_weight_ref,
    pre_weight_ref,
    solved_ref,
    inverse_rows_ref,
    load_rows_ref,
    coupling_rows_ref,
    picked_ref,
    picked_weight_ref,
    incoming_ref,
    term_pay_ref,
    term_got_ref,
    pick_pay_ref,
    pick_got_ref,
    weight_pay_ref,
    weight_got_ref,
    term_send,
    term_recv,
    last_send,
    last_recv,
):
    slots, modes, inner, columns, owned, shared, windows, pad, span = sizes
    groups = slots // GS
    own_windows = owned // GS
    starts = [min(k * shared // GS, windows - own_windows - span) for k in range(4)]
    shifts = [k * shared - GS * starts[k] for k in range(4)]
    group = pl.program_id(0)
    halves = columns // LANES
    nx, ny = counts
    a, b = lax.axis_index("px"), lax.axis_index("py")
    targets = (
        (lax.rem(a + nx - 1, nx), b),
        (lax.rem(a + 1, nx), b),
        (a, lax.rem(b + ny - 1, ny)),
        (a, lax.rem(b + 1, ny)),
    )

    @pl.when(group == 0)
    def _():
        barrier = pltpu.get_barrier_semaphore()
        for target in targets:
            pl.semaphore_signal(
                barrier, inc=1, device_id=target, device_id_type=pl.DeviceIdType.MESH
            )
        solved_ref[...] = jnp.zeros_like(solved_ref)
        picked_ref[...] = jnp.zeros_like(picked_ref)
        picked_weight_ref[...] = jnp.ones_like(picked_weight_ref)
        pl.semaphore_wait(barrier, 4)

    def remote(source, dest, send_sem, recv_sem, k):
        return pltpu.make_async_remote_copy(
            src_ref=source,
            dst_ref=dest,
            send_sem=send_sem,
            recv_sem=recv_sem,
            device_id=targets[k],
            device_id_type=pl.DeviceIdType.MESH,
        )

    def term_copy(k, g):
        o = OPPOSITE[k]
        return remote(
            term_pay_ref.at[k, g], term_got_ref.at[o, g], term_send.at[k, g], term_recv.at[o, g], k
        )

    def pick_copy(k):
        o = OPPOSITE[k]
        return remote(
            pick_pay_ref.at[k], pick_got_ref.at[o], last_send.at[0, k], last_recv.at[0, o], k
        )

    def weight_copy(k):
        o = OPPOSITE[k]
        return remote(
            weight_pay_ref.at[k], weight_got_ref.at[o], last_send.at[1, k], last_recv.at[1, o], k
        )

    count = count_ref[0, 0]
    lane = lax.broadcasted_iota(jnp.int32, (modes, LANES), 1)
    window_ids = lax.broadcasted_iota(jnp.int32, (windows, modes), 0)
    weight_cols = weight_ref[...].T
    window_of = dof_ref[...] // GS
    inverse_rows_ref[:, :inner] = inverse_ref[...].astype(jnp.float32).reshape(inner * GS, inner)
    coupling_rows_ref[:, :inner] = (
        coupling_ref[...].astype(jnp.float32).reshape(modes * GS, inner)
    )
    load_rows = load_ref[...].astype(jnp.float32).reshape(inner * GS, columns)
    for c in range(halves):
        load_rows_ref[c] = load_rows[:, c * LANES : (c + 1) * LANES]
    weight_total = jnp.zeros((windows, LANES), jnp.float32)
    for e in range(GS):
        live = group * GS + e < count
        inverse = inverse_rows_ref[pl.ds(e, inner, stride=GS), :][:, :inner].astype(jnp.bfloat16)
        load = jnp.concatenate(
            [load_rows_ref[c, pl.ds(e, inner, stride=GS), :] for c in range(halves)], axis=1
        ).astype(jnp.bfloat16)
        inverse_out_ref[e] = inverse
        load_out_ref[e] = load
        solved = jnp.dot(inverse, load, preferred_element_type=jnp.float32)
        solved = jnp.where(live, solved, 0.0).astype(jnp.bfloat16)
        solved_ref[e, :inner, :] = solved
        col = jnp.where(live, weight_cols[:, e : e + 1], 0.0)
        high = col.astype(jnp.bfloat16).astype(jnp.float32)
        mid = (col - high).astype(jnp.bfloat16).astype(jnp.float32)
        low = col - high - mid
        extra = jnp.where(lane == inner, high, jnp.where(lane == inner + 1, mid, low))
        ext = jnp.where(
            lane < inner, coupling_rows_ref[pl.ds(e, modes, stride=GS), :], extra
        ).astype(jnp.bfloat16)
        onehot = (window_ids == window_of[e : e + 1, :]).astype(jnp.bfloat16)
        spread = jnp.dot(onehot, ext, preferred_element_type=jnp.float32)
        weight_total = weight_total + spread
        spread_ref[:, e * LANES : (e + 1) * LANES] = spread.astype(jnp.bfloat16)

    rows = jnp.dot(
        spread_ref[...],
        solved_ref[...].reshape(GS * LANES, columns),
        preferred_element_type=jnp.float32,
    )
    for k in range(4):
        at = own_windows + starts[k]
        term_pay_ref[k, group] = rows[at : at + span].astype(jnp.bfloat16)
        term_copy(k, group).start()
    wide_lane = lax.broadcasted_iota(jnp.int32, (windows, LANES), 1)
    weight_sum = jnp.sum(jnp.where(wide_lane >= inner, weight_total, 0.0), axis=1, keepdims=True)
    for c in range(halves):
        local_ref[c, pl.ds(group, windows, stride=GS), :] = rows[:, c * LANES : (c + 1) * LANES]
    local_weight_ref[pl.ds(group, windows, stride=GS), :] = jnp.broadcast_to(
        weight_sum, (windows, LANES)
    )

    @pl.when(group == groups - 1)
    def _():
        def subtract(chunk, carry):
            at = pl.ds(pl.multiple_of(chunk * LANES, LANES), LANES)
            for c in range(halves):
                values_ref[c, at, :] = (
                    edge_ref[at, c * LANES : (c + 1) * LANES].astype(jnp.float32)
                    - local_ref[c, at, :]
                )
            own = jnp.broadcast_to(owner_ref[pl.ds(chunk, 1), :], (LANES, LANES)).T
            pre_weight_ref[at, :] = own + local_weight_ref[at, :]
            return carry

        lax.fori_loop(0, owned // LANES, subtract, 0)

        for pair in ((0, 1), (2, 3)):

            def pick(s, carry):
                loaded = []
                for k in pair:
                    r = readers_ref[k, s]
                    loaded.append(
                        (
                            [values_ref[c, pl.ds(r, 1), :] for c in range(halves)],
                            pre_weight_ref[pl.ds(r, 1), :],
                        )
                    )
                for k, (values, weight) in zip(pair, loaded):
                    for c in range(halves):
                        picked_ref[k, c, pl.ds(s, 1), :] = values[c]
                    picked_weight_ref[k, pl.ds(s, 1), :] = weight
                return carry

            lax.fori_loop(0, shared, pick, 0, unroll=6)
            for k in pair:
                for c in range(halves):
                    pick_pay_ref[k, :, c * LANES : (c + 1) * LANES] = picked_ref[k, c].astype(
                        jnp.bfloat16
                    )
                pick_copy(k).start()
                start = owned + k * shared
                sub = lax.broadcasted_iota(jnp.int32, (8, pad), 0)
                weight_pay_ref[k] = jnp.where(
                    sub == 0,
                    local_weight_ref[start : start + pad, :].T[:8],
                    picked_weight_ref[k].T[:8],
                )
                weight_copy(k).start()

        def divide(chunk, carry):
            at = pl.ds(pl.multiple_of(chunk * LANES, LANES), LANES)
            scale = 1.0 / pre_weight_ref[at, :]
            for c in range(halves):
                values_ref[c, at, :] = values_ref[c, at, :] * scale
            return carry

        lax.fori_loop(0, owned // LANES, divide, 0)
        tail = owned + 4 * shared
        if windows * GS > tail:
            for c in range(halves):
                values_ref[c, tail:, :] = jnp.zeros((windows * GS - tail, LANES), jnp.float32)

        for k in range(4):

            def settle(g, carry):
                term_copy(k, g).wait()
                return carry

            lax.fori_loop(0, groups, settle, 0)
        for k in range(4):
            for g in range(groups):
                piece = term_got_ref[k, g].astype(jnp.float32)
                for c in range(halves):
                    incoming_ref[k, c, pl.ds(g, span, stride=GS), :] = piece[
                        :, c * LANES : (c + 1) * LANES
                    ]
        for k in (2, 3, 0, 1):
            pick_copy(k).wait_send()
            weight_copy(k).wait_send()
        for k in (3, 2, 1, 0):
            pick_copy(k).wait_recv()
            weight_copy(k).wait_recv()
        for k in range(4):
            weights = weight_got_ref[k].T
            start = owned + k * shared
            to_mine = 1.0 / (picked_weight_ref[k] + weights[:, 0:1])
            to_theirs = 1.0 / (local_weight_ref[start : start + pad, :] + weights[:, 1:2])
            shift = shifts[OPPOSITE[k]]
            for c in range(halves):
                cols = slice(c * LANES, (c + 1) * LANES)
                ready_ref[k, c] = (
                    picked_ref[k, c] - incoming_ref[k, c, shift : shift + pad, :]
                ) * to_mine
                theirs = (
                    pick_got_ref[k, :, cols].astype(jnp.float32)
                    - local_ref[c, start : start + pad, :]
                ) * to_theirs
                values_ref[c, start : start + shared, :] = theirs[:shared]


def recover_kernel(
    sizes,
    count_ref,
    readers_ref,
    values_in_ref,
    ready_ref,
    spread_ref,
    inverse_ref,
    load_ref,
    face_ref,
    out_ref,
    values_ref,
    out_rows_ref,
    in_sem,
    face_sem,
):
    slots, modes, inner, columns, owned, shared, windows, pad, span = sizes
    group = pl.program_id(0)
    halves = columns // LANES
    groups = slots // GS

    def face_copy(c):
        return pltpu.make_async_copy(
            values_ref.at[c, pl.ds(0, owned)],
            face_ref.at[0, 0, :, pl.ds(c * LANES, LANES)],
            face_sem.at[c],
        )

    @pl.when(group == 0)
    def _():
        fetch = pltpu.make_async_copy(values_in_ref, values_ref, in_sem)
        fetch.start()
        fetch.wait()

        def place(s, carry):
            loaded = []
            for k in range(4):
                loaded.append([ready_ref[k, c, pl.ds(s, 1), :] for c in range(halves)])
            for k in range(4):
                r = readers_ref[k, s]
                for c in range(halves):
                    values_ref[c, pl.ds(r, 1), :] = loaded[k][c]
            return carry

        lax.fori_loop(0, shared, place, 0, unroll=4)
        for c in range(halves):
            face_copy(c).start()

    table = jnp.concatenate(
        [values_ref[c, pl.ds(group, windows, stride=GS), :] for c in range(halves)], axis=1
    )
    turned = table.T.astype(jnp.bfloat16)
    pulled_turned = jnp.dot(turned, spread_ref[...], preferred_element_type=jnp.float32)
    count = count_ref[0, 0]
    for e in range(GS):
        live = group * GS + e < count
        pulled = pulled_turned[:, e * LANES : (e + 1) * LANES].T[:inner]
        reduced = (load_ref[e].astype(jnp.float32) - pulled).astype(jnp.bfloat16)
        result = jnp.dot(inverse_ref[e], reduced, preferred_element_type=jnp.float32)
        result = jnp.where(live, result, 0.0)
        for c in range(halves):
            out_rows_ref[c, pl.ds(e, inner, stride=GS), :] = result[:, c * LANES : (c + 1) * LANES]
    out_ref[...] = (
        jnp.concatenate([out_rows_ref[c] for c in range(halves)], axis=1)
        .reshape(inner, GS, columns)
        .astype(jnp.bfloat16)
    )

    @pl.when(group == groups - 1)
    def _():
        for c in range(halves):
            face_copy(c).wait()


def per_device(
    counts,
    coupling,
    interior_inverse,
    interior_load,
    boundary_load,
    owner_weight,
    elem_weight,
    elem_dof,
    reader_rows,
    elem_count,
):
    slots, modes, inner = coupling.shape[2:]
    columns = interior_load.shape[-1]
    owned = boundary_load.shape[2]
    shared = reader_rows.shape[3]
    groups = slots // GS
    halves = columns // LANES
    windows = round_up((owned + 4 * shared) // GS, 16)
    pad = round_up(shared, 16)
    span = round_up(shared // GS + 2, 16)
    sizes = (slots, modes, inner, columns, owned, shared, windows, pad, span)
    f32, bf16 = jnp.float32, jnp.bfloat16
    smem = pl.BlockSpec(memory_space=pltpu.SMEM)
    vmem = pl.BlockSpec(memory_space=pltpu.VMEM)
    anyplace = pl.BlockSpec(memory_space=pl.ANY)

    def by_group(*tail):
        zeros = (0,) * len(tail)
        return pl.BlockSpec((None, None, GS) + tail, lambda g: (0, 0, g) + zeros)

    def by_mode(rows, width):
        return pl.BlockSpec((None, None, rows, GS, width), lambda g: (0, 0, 0, g, 0))

    def by_slot(rows, width):
        return pl.BlockSpec((GS, rows, width), lambda g: (g, 0, 0))

    def modes_first(array):
        return jnp.swapaxes(array, 2, 3)

    spread_spec = pl.BlockSpec((None, windows, GS * LANES), lambda g: (g, 0, 0))
    readers = reader_rows[0, 0]
    params = dict(vmem_limit_bytes=VMEM_BYTES, dimension_semantics=("arbitrary",))
    shape = jax.ShapeDtypeStruct
    spread, inverse_rows, load_rows, values, ready = pl.pallas_call(
        functools.partial(condense_kernel, sizes, counts),
        grid=(groups,),
        in_specs=[
            smem,
            smem,
            by_mode(inner, inner),
            by_mode(inner, columns),
            by_mode(modes, inner),
            by_group(modes),
            by_group(modes),
            vmem,
            vmem,
        ],
        out_specs=[spread_spec, by_slot(inner, inner), by_slot(inner, columns), vmem, vmem],
        out_shape=[
            shape((groups, windows, GS * LANES), bf16),
            shape((slots, inner, inner), bf16),
            shape((slots, inner, columns), bf16),
            shape((halves, windows * GS, LANES), f32),
            shape((4, halves, pad, LANES), f32),
        ],
        scratch_shapes=[
            pltpu.VMEM((halves, windows * GS, LANES), f32),
            pltpu.VMEM((windows * GS, LANES), f32),
            pltpu.VMEM((owned, LANES), f32),
            pltpu.VMEM((GS, LANES, columns), bf16),
            pltpu.VMEM((inner * GS, LANES), f32),
            pltpu.VMEM((halves, inner * GS, LANES), f32),
            pltpu.VMEM((modes * GS, LANES), f32),
            pltpu.VMEM((4, halves, pad, LANES), f32),
            pltpu.VMEM((4, pad, LANES), f32),
            pltpu.VMEM((4, halves, span * GS, LANES), f32),
            pltpu.VMEM((4, groups, span, columns), bf16),
            pltpu.VMEM((4, groups, span, columns), bf16),
            pltpu.VMEM((4, pad, columns), bf16),
            pltpu.VMEM((4, pad, columns), bf16),
            pltpu.VMEM((4, 8, pad), f32),
            pltpu.VMEM((4, 8, pad), f32),
            pltpu.SemaphoreType.DMA((4, groups)),
            pltpu.SemaphoreType.DMA((4, groups)),
            pltpu.SemaphoreType.DMA((2, 4)),
            pltpu.SemaphoreType.DMA((2, 4)),
        ],
        compiler_params=pltpu.CompilerParams(
            collective_id=0, has_side_effects=True, **params
        ),
        name="condense",
    )(
        elem_count,
        readers,
        modes_first(interior_inverse),
        modes_first(interior_load),
        modes_first(coupling),
        elem_weight,
        elem_dof,
        boundary_load[0, 0],
        owner_weight.reshape(owned // LANES, LANES),
    )
    face, interior = pl.pallas_call(
        functools.partial(recover_kernel, sizes),
        grid=(groups,),
        in_specs=[
            smem,
            smem,
            anyplace,
            vmem,
            spread_spec,
            by_slot(inner, inner),
            by_slot(inner, columns),
        ],
        out_specs=[anyplace, by_mode(inner, columns)],
        out_shape=[
            shape((1, 1, owned, columns), f32),
            shape((1, 1, inner, slots, columns), bf16),
        ],
        scratch_shapes=[
            pltpu.VMEM((halves, windows * GS, LANES), f32),
            pltpu.VMEM((halves, inner * GS, LANES), f32),
            pltpu.SemaphoreType.DMA,
            pltpu.SemaphoreType.DMA((halves,)),
        ],
        compiler_params=pltpu.CompilerParams(**params),
        name="recover",
    )(elem_count, readers, values, ready, spread, inverse_rows, load_rows)
    return face, modes_first(interior)


def solution(mesh):
    in_specs = (
        P("px", "py", None, None, None),
        P("px", "py", None, None, None),
        P("px", "py", None, None, None),
        P("px", "py", None, None),
        P("px", "py", None),
        P("px", "py", None, None),
        P("px", "py", None, None),
        P("px", "py", None, None),
        P("px", "py"),
    )
    out_specs = (P("px", "py", None, None), P("px", "py", None, None, None))
    counts = (mesh.shape["px"], mesh.shape["py"])
    return jax.shard_map(
        functools.partial(per_device, counts),
        mesh=mesh,
        in_specs=in_specs,
        out_specs=out_specs,
        check_vma=False,
    )
```

```python
import functools

import jax
import jax.numpy as jnp
from jax import lax
from jax.experimental import pallas as pl
from jax.experimental.pallas import tpu as pltpu
from jax.sharding import PartitionSpec as P

GS = 8
LANES = 128
VMEM_BYTES = 58 * 2**20
OPPOSITE = (1, 0, 3, 2)


def round_up(value, unit):
    return (value + unit - 1) // unit * unit


def condense_kernel(
    sizes,
    counts,
    count_ref,
    readers_ref,
    inverse_ref,
    load_ref,
    coupling_ref,
    weight_ref,
    dof_ref,
    edge_ref,
    owner_ref,
    reader_rows_ref,
    turned_ref,
    inverse_out_ref,
    load_out_ref,
    face_ref,
    part_ref,
    shared_ref,
    values_ref,
    spread_ref,
    local_ref,
    local_weight_ref,
    pre_weight_ref,
    solved_ref,
    inverse_rows_ref,
    load_rows_ref,
    coupling_rows_ref,
    picked_ref,
    picked_weight_ref,
    incoming_ref,
    added_ref,
    reader_lane_ref,
    added_weight_ref,
    theirs_ref,
    term_pay_ref,
    term_got_ref,
    pick_pay_ref,
    pick_got_ref,
    weight_pay_ref,
    weight_got_ref,
    term_send,
    term_recv,
    last_send,
    last_recv,
    face_sem,
):
    slots, modes, inner, columns, owned, shared, windows, pad, lanes, span = sizes
    groups = slots // GS
    own_windows = owned // GS
    starts = [min(k * shared // GS, windows - own_windows - span) for k in range(4)]
    shifts = [k * shared - GS * starts[k] for k in range(4)]
    step = pl.program_id(0)
    group = lax.rem(step, groups)
    halves = columns // LANES
    nx, ny = counts
    a, b = lax.axis_index("px"), lax.axis_index("py")
    targets = (
        (lax.rem(a + nx - 1, nx), b),
        (lax.rem(a + 1, nx), b),
        (a, lax.rem(b + ny - 1, ny)),
        (a, lax.rem(b + 1, ny)),
    )

    @pl.when(step == 0)
    def _():
        barrier = pltpu.get_barrier_semaphore()
        for target in targets:
            pl.semaphore_signal(
                barrier, inc=1, device_id=target, device_id_type=pl.DeviceIdType.MESH
            )
        solved_ref[...] = jnp.zeros_like(solved_ref)
        picked_ref[...] = jnp.zeros_like(picked_ref)
        picked_weight_ref[...] = jnp.ones_like(picked_weight_ref)
        added_ref[...] = jnp.zeros_like(added_ref)
        reader_lane_ref[...] = jnp.full_like(reader_lane_ref, -1)
        for k in range(4):
            reader_lane_ref[:1, k * lanes : k * lanes + shared] = reader_rows_ref[k : k + 1, :]
        pl.semaphore_wait(barrier, 4)

    def remote(source, dest, send_sem, recv_sem, k):
        return pltpu.make_async_remote_copy(
            src_ref=source,
            dst_ref=dest,
            send_sem=send_sem,
            recv_sem=recv_sem,
            device_id=targets[k],
            device_id_type=pl.DeviceIdType.MESH,
        )

    def term_copy(k, g):
        o = OPPOSITE[k]
        return remote(
            term_pay_ref.at[k, g], term_got_ref.at[o, g], term_send.at[k, g], term_recv.at[o, g], k
        )

    def pick_copy(k):
        o = OPPOSITE[k]
        return remote(
            pick_pay_ref.at[k], pick_got_ref.at[o], last_send.at[0, k], last_recv.at[0, o], k
        )

    def weight_copy(part, k):
        o = OPPOSITE[k]
        return remote(
            weight_pay_ref.at[part, k],
            weight_got_ref.at[part, o],
            last_send.at[part + 1, k],
            last_recv.at[part + 1, o],
            k,
        )

    def face_copy(c):
        return pltpu.make_async_copy(
            values_ref.at[c],
            face_ref.at[0, 0, :, pl.ds(c * LANES, LANES)],
            face_sem.at[c],
        )

    @pl.when(step < groups)
    def _():
        count = count_ref[0, 0]
        lane = lax.broadcasted_iota(jnp.int32, (modes, LANES), 1)
        window_ids = lax.broadcasted_iota(jnp.int32, (windows, modes), 0)
        weight_cols = weight_ref[...].T
        window_of = dof_ref[...] // GS
        inverse_rows_ref[:, :inner] = inverse_ref[...].astype(jnp.float32).reshape(inner * GS, inner)
        coupling_rows_ref[:, :inner] = (
            coupling_ref[...].astype(jnp.float32).reshape(modes * GS, inner)
        )
        load_rows = load_ref[...].astype(jnp.float32).reshape(inner * GS, columns)
        for c in range(halves):
            load_rows_ref[c] = load_rows[:, c * LANES : (c + 1) * LANES]
        weight_total = jnp.zeros((windows, LANES), jnp.float32)
        for e in range(GS):
            live = group * GS + e < count
            inverse = inverse_rows_ref[pl.ds(e, inner, stride=GS), :][:, :inner].astype(jnp.bfloat16)
            load = jnp.concatenate(
                [load_rows_ref[c, pl.ds(e, inner, stride=GS), :] for c in range(halves)], axis=1
            ).astype(jnp.bfloat16)
            inverse_out_ref[e] = inverse
            load_out_ref[e] = load
            solved = jnp.dot(inverse, load, preferred_element_type=jnp.float32)
            solved = jnp.where(live, solved, 0.0).astype(jnp.bfloat16)
            solved_ref[e, :inner, :] = solved
            col = jnp.where(live, weight_cols[:, e : e + 1], 0.0)
            high = col.astype(jnp.bfloat16).astype(jnp.float32)
            mid = (col - high).astype(jnp.bfloat16).astype(jnp.float32)
            low = col - high - mid
            extra = jnp.where(lane == inner, high, jnp.where(lane == inner + 1, mid, low))
            ext = jnp.where(
                lane < inner, coupling_rows_ref[pl.ds(e, modes, stride=GS), :], extra
            ).astype(jnp.bfloat16)
            onehot = (window_ids == window_of[e : e + 1, :]).astype(jnp.bfloat16)
            spread = jnp.dot(onehot, ext, preferred_element_type=jnp.float32)
            weight_total = weight_total + spread
            spread_ref[group, :, e * LANES : (e + 1) * LANES] = spread.astype(jnp.bfloat16)

        rows = jnp.dot(
            spread_ref[group],
            solved_ref[...].reshape(GS * LANES, columns),
            preferred_element_type=jnp.float32,
        )
        turned_ref[...] = spread_ref[group, own_windows:, :].T
        for k in range(4):
            at = own_windows + starts[k]
            term_pay_ref[k, group] = rows[at : at + span].astype(jnp.bfloat16)
            term_copy(k, group).start()
        wide_lane = lax.broadcasted_iota(jnp.int32, (windows, LANES), 1)
        weight_sum = jnp.sum(jnp.where(wide_lane >= inner, weight_total, 0.0), axis=1, keepdims=True)
        for c in range(halves):
            local_ref[c, pl.ds(group, windows, stride=GS), :] = rows[:, c * LANES : (c + 1) * LANES]
        local_weight_ref[pl.ds(group, windows, stride=GS), :] = jnp.broadcast_to(
            weight_sum, (windows, LANES)
        )

    @pl.when(step == groups - 1)
    def _():
        for k in range(4):
            start = owned + k * shared
            weight_pay_ref[0, k] = local_weight_ref[start : start + lanes, :].T[:8]
            weight_copy(0, k).start()

        def subtract(chunk, carry):
            at = pl.ds(pl.multiple_of(chunk * LANES, LANES), LANES)
            for c in range(halves):
                values_ref[c, at, :] = (
                    edge_ref[at, c * LANES : (c + 1) * LANES].astype(jnp.float32)
                    - local_ref[c, at, :]
                )
            own = jnp.broadcast_to(owner_ref[:, at], (LANES, LANES)).T
            pre_weight_ref[at, :] = own + local_weight_ref[at, :]
            return carry

        lax.fori_loop(0, owned // LANES, subtract, 0, unroll=4)

        for pair in ((0, 1), (2, 3)):

            def pick(s, carry):
                loaded = []
                for k in pair:
                    r = readers_ref[k, s]
                    loaded.append(
                        (
                            [values_ref[c, pl.ds(r, 1), :] for c in range(halves)],
                            pre_weight_ref[pl.ds(r, 1), :],
                        )
                    )
                for k, (values, weight) in zip(pair, loaded):
                    for c in range(halves):
                        picked_ref[k, c, pl.ds(s, 1), :] = values[c]
                    picked_weight_ref[k, pl.ds(s, 1), :] = weight
                return carry

            lax.fori_loop(0, shared, pick, 0, unroll=6)
            for k in pair:
                for c in range(halves):
                    pick_pay_ref[k, :, c * LANES : (c + 1) * LANES] = picked_ref[k, c].astype(
                        jnp.bfloat16
                    )
                pick_copy(k).start()
                weight_pay_ref[1, k] = picked_weight_ref[k].T[:8]
                weight_copy(1, k).start()

        for k in range(4):

            def settle(g, carry):
                term_copy(k, g).wait()
                return carry

            lax.fori_loop(0, groups, settle, 0)
            weight_copy(0, k).wait()
        for k in range(4):
            for g in range(groups):
                piece = term_got_ref[k, g].astype(jnp.float32)
                for c in range(halves):
                    incoming_ref[k, c, pl.ds(g, span, stride=GS), :] = piece[
                        :, c * LANES : (c + 1) * LANES
                    ]
            shift = shifts[OPPOSITE[k]]
            for c in range(halves):
                added_ref[k * lanes : k * lanes + pad, c * LANES : (c + 1) * LANES] = incoming_ref[
                    k, c, shift : shift + pad, :
                ].astype(jnp.bfloat16)
            added_weight_ref[:1, k * lanes : (k + 1) * lanes] = weight_got_ref[0, k, :1, :]

        row_ids = lax.broadcasted_iota(jnp.int32, (2 * LANES, 4 * lanes), 0)

        def finish(chunk, carry):
            at = pl.ds(pl.multiple_of(chunk * 2 * LANES, 2 * LANES), 2 * LANES)
            hit = row_ids == reader_lane_ref[:1, :] - chunk * 2 * LANES
            added = jnp.dot(
                hit.astype(jnp.bfloat16), added_ref[...], preferred_element_type=jnp.float32
            )
            weight = jnp.sum(
                jnp.where(hit, added_weight_ref[:1, :], 0.0), axis=1, keepdims=True
            )
            scale = 1.0 / (pre_weight_ref[at, :] + weight)
            for c in range(halves):
                values_ref[c, at, :] = (
                    values_ref[c, at, :] - added[:, c * LANES : (c + 1) * LANES]
                ) * scale
            return carry

        lax.fori_loop(0, owned // (2 * LANES), finish, 0)
        for c in range(halves):
            face_copy(c).start()

    @pl.when(step >= groups)
    def _():
        table = jnp.concatenate(
            [values_ref[c, pl.ds(group, own_windows, stride=GS), :] for c in range(halves)], axis=1
        )
        part_ref[...] = jnp.dot(
            table.T.astype(jnp.bfloat16),
            spread_ref[group, :own_windows, :],
            preferred_element_type=jnp.float32,
        ).T

    @pl.when(step == 2 * groups - 1)
    def _():
        for k in range(4):
            pick_copy(k).wait()
            weight_copy(1, k).wait()
        theirs_ref[...] = jnp.zeros_like(theirs_ref)
        for k in range(4):
            weights = weight_got_ref[1, k].T
            start = owned + k * shared
            scale = 1.0 / (local_weight_ref[start : start + pad, :] + weights[:pad, 0:1])
            for c in range(halves):
                theirs = (
                    pick_got_ref[k, :, c * LANES : (c + 1) * LANES].astype(jnp.float32)
                    - local_ref[c, start : start + pad, :]
                ) * scale
                theirs_ref[c, k * shared : (k + 1) * shared, :] = theirs[:shared]
        for g in range(groups):
            for c in range(halves):
                shared_ref[g, :, c * LANES : (c + 1) * LANES] = theirs_ref[
                    c, pl.ds(g, windows - own_windows, stride=GS), :
                ].astype(jnp.bfloat16)
        for c in range(halves):
            face_copy(c).wait()


def recover_kernel(
    sizes,
    count_ref,
    face_in_ref,
    turned_ref,
    shared_ref,
    part_ref,
    inverse_ref,
    load_ref,
    face_ref,
    out_ref,
    out_rows_ref,
    face_sem,
):
    slots, modes, inner, columns, owned, shared, windows, pad, lanes, span = sizes
    group = pl.program_id(0)
    halves = columns // LANES
    groups = slots // GS

    @pl.when(group == 0)
    def _():
        pltpu.make_async_copy(face_in_ref, face_ref, face_sem).start()

    pulled = part_ref[...] + jnp.dot(
        turned_ref[...], shared_ref[group], preferred_element_type=jnp.float32
    )
    count = count_ref[0, 0]
    for e in range(GS):
        live = group * GS + e < count
        reduced = (
            load_ref[e].astype(jnp.float32) - pulled[e * LANES : e * LANES + inner]
        ).astype(jnp.bfloat16)
        result = jnp.dot(inverse_ref[e], reduced, preferred_element_type=jnp.float32)
        result = jnp.where(live, result, 0.0)
        for c in range(halves):
            out_rows_ref[c, pl.ds(e, inner, stride=GS), :] = result[:, c * LANES : (c + 1) * LANES]
    out_ref[...] = (
        jnp.concatenate([out_rows_ref[c] for c in range(halves)], axis=1)
        .reshape(inner, GS, columns)
        .astype(jnp.bfloat16)
    )

    @pl.when(group == groups - 1)
    def _():
        pltpu.make_async_copy(face_in_ref, face_ref, face_sem).wait()


def per_device(
    counts,
    coupling,
    interior_inverse,
    interior_load,
    boundary_load,
    owner_weight,
    elem_weight,
    elem_dof,
    reader_rows,
    elem_count,
):
    slots, modes, inner = coupling.shape[2:]
    columns = interior_load.shape[-1]
    owned = boundary_load.shape[2]
    shared = reader_rows.shape[3]
    groups = slots // GS
    halves = columns // LANES
    windows = round_up((owned + 4 * shared) // GS, 16)
    pad = round_up(shared, 16)
    span = round_up(shared // GS + 2, 16)
    lanes = round_up(shared, LANES)
    own_windows = owned // GS
    shared_windows = windows - own_windows
    sizes = (slots, modes, inner, columns, owned, shared, windows, pad, lanes, span)
    f32, bf16 = jnp.float32, jnp.bfloat16
    smem = pl.BlockSpec(memory_space=pltpu.SMEM)
    vmem = pl.BlockSpec(memory_space=pltpu.VMEM)
    anyplace = pl.BlockSpec(memory_space=pl.ANY)

    def at_first(g):
        return jnp.minimum(g, groups - 1)

    def by_group(*tail):
        zeros = (0,) * len(tail)
        return pl.BlockSpec((None, None, GS) + tail, lambda g: (0, 0, at_first(g)) + zeros)

    def by_mode(rows, width):
        return pl.BlockSpec(
            (None, None, rows, GS, width), lambda g: (0, 0, 0, at_first(g), 0)
        )

    def by_slot(rows, width):
        return pl.BlockSpec((GS, rows, width), lambda g: (at_first(g), 0, 0))

    def modes_first(array):
        return jnp.swapaxes(array, 2, 3)

    turned_spec = pl.BlockSpec(
        (None, GS * LANES, shared_windows), lambda g: (at_first(g), 0, 0)
    )
    part_block = (None, GS * LANES, columns)
    readers = reader_rows[0, 0]
    params = dict(vmem_limit_bytes=VMEM_BYTES, dimension_semantics=("arbitrary",))
    shape = jax.ShapeDtypeStruct
    turned, inverse_rows, load_rows, face_mid, part, shared_values = pl.pallas_call(
        functools.partial(condense_kernel, sizes, counts),
        grid=(2 * groups,),
        in_specs=[
            smem,
            smem,
            by_mode(inner, inner),
            by_mode(inner, columns),
            by_mode(modes, inner),
            by_group(modes),
            by_group(modes),
            vmem,
            vmem,
            vmem,
        ],
        out_specs=[
            turned_spec,
            by_slot(inner, inner),
            by_slot(inner, columns),
            anyplace,
            pl.BlockSpec(part_block, lambda g: (jnp.maximum(g - groups, 0), 0, 0)),
            vmem,
        ],
        out_shape=[
            shape((groups, GS * LANES, shared_windows), bf16),
            shape((slots, inner, inner), bf16),
            shape((slots, inner, columns), bf16),
            shape((1, 1, owned, columns), f32),
            shape((groups, GS * LANES, columns), f32),
            shape((groups, shared_windows, columns), bf16),
        ],
        scratch_shapes=[
            pltpu.VMEM((halves, owned, LANES), f32),
            pltpu.VMEM((groups, windows, GS * LANES), bf16),
            pltpu.VMEM((halves, windows * GS, LANES), f32),
            pltpu.VMEM((windows * GS + LANES, LANES), f32),
            pltpu.VMEM((owned, LANES), f32),
            pltpu.VMEM((GS, LANES, columns), bf16),
            pltpu.VMEM((inner * GS, LANES), f32),
            pltpu.VMEM((halves, inner * GS, LANES), f32),
            pltpu.VMEM((modes * GS, LANES), f32),
            pltpu.VMEM((4, halves, pad, LANES), f32),
            pltpu.VMEM((4, lanes, LANES), f32),
            pltpu.VMEM((4, halves, span * GS, LANES), f32),
            pltpu.VMEM((4 * lanes, columns), bf16),
            pltpu.VMEM((8, 4 * lanes), jnp.int32),
            pltpu.VMEM((8, 4 * lanes), f32),
            pltpu.VMEM((halves, shared_windows * GS, LANES), f32),
            pltpu.VMEM((4, groups, span, columns), bf16),
            pltpu.VMEM((4, groups, span, columns), bf16),
            pltpu.VMEM((4, pad, columns), bf16),
            pltpu.VMEM((4, pad, columns), bf16),
            pltpu.VMEM((2, 4, 8, lanes), f32),
            pltpu.VMEM((2, 4, 8, lanes), f32),
            pltpu.SemaphoreType.DMA((4, groups)),
            pltpu.SemaphoreType.DMA((4, groups)),
            pltpu.SemaphoreType.DMA((3, 4)),
            pltpu.SemaphoreType.DMA((3, 4)),
            pltpu.SemaphoreType.DMA((halves,)),
        ],
        compiler_params=pltpu.CompilerParams(
            collective_id=0, has_side_effects=True, **params
        ),
        name="condense",
    )(
        elem_count,
        readers,
        modes_first(interior_inverse),
        modes_first(interior_load),
        modes_first(coupling),
        elem_weight,
        elem_dof,
        boundary_load[0, 0],
        owner_weight[0],
        readers,
    )
    face, interior = pl.pallas_call(
        functools.partial(recover_kernel, sizes),
        grid=(groups,),
        in_specs=[
            smem,
            anyplace,
            turned_spec,
            vmem,
            pl.BlockSpec(part_block, lambda g: (g, 0, 0)),
            by_slot(inner, inner),
            by_slot(inner, columns),
        ],
        out_specs=[anyplace, by_mode(inner, columns)],
        out_shape=[
            shape((1, 1, owned, columns), f32),
            shape((1, 1, inner, slots, columns), bf16),
        ],
        scratch_shapes=[
            pltpu.VMEM((halves, inner * GS, LANES), f32),
            pltpu.SemaphoreType.DMA,
        ],
        compiler_params=pltpu.CompilerParams(**params),
        name="recover",
    )(elem_count, face_mid, turned, shared_values, part, inverse_rows, load_rows)
    return face, modes_first(interior)


def solution(mesh):
    in_specs = (
        P("px", "py", None, None, None),
        P("px", "py", None, None, None),
        P("px", "py", None, None, None),
        P("px", "py", None, None),
        P("px", "py", None),
        P("px", "py", None, None),
        P("px", "py", None, None),
        P("px", "py", None, None),
        P("px", "py"),
    )
    out_specs = (P("px", "py", None, None), P("px", "py", None, None, None))
    counts = (mesh.shape["px"], mesh.shape["py"])
    return jax.shard_map(
        functools.partial(per_device, counts),
        mesh=mesh,
        in_specs=in_specs,
        out_specs=out_specs,
        check_vma=False,
    )
```

```python
import functools

import jax
import jax.numpy as jnp
from jax import lax
from jax.experimental import pallas as pl
from jax.experimental.pallas import tpu as pltpu
from jax.sharding import PartitionSpec as P

GS = 8
LANES = 128
VMEM_BYTES = 58 * 2**20
OPPOSITE = (1, 0, 3, 2)


def round_up(value, unit):
    return (value + unit - 1) // unit * unit


def condense_kernel(
    sizes,
    counts,
    count_ref,
    readers_ref,
    inverse_ref,
    load_ref,
    coupling_ref,
    weight_ref,
    dof_ref,
    edge_ref,
    owner_ref,
    reader_rows_ref,
    turned_ref,
    inverse_out_ref,
    load_out_ref,
    face_ref,
    part_ref,
    shared_ref,
    values_ref,
    spread_ref,
    local_ref,
    local_weight_ref,
    pre_weight_ref,
    solved_ref,
    inverse_rows_ref,
    load_rows_ref,
    coupling_rows_ref,
    picked_ref,
    picked_weight_ref,
    incoming_ref,
    added_ref,
    reader_lane_ref,
    theirs_ref,
    term_pay_ref,
    term_got_ref,
    pick_pay_ref,
    pick_got_ref,
    weight_pay_ref,
    weight_got_ref,
    term_send,
    term_recv,
    last_send,
    last_recv,
    face_sem,
):
    slots, modes, inner, columns, owned, shared, windows, pad, lanes, span = sizes
    groups = slots // GS
    own_windows = owned // GS
    starts = [min(k * shared // GS, windows - own_windows - span) for k in range(4)]
    shifts = [k * shared - GS * starts[k] for k in range(4)]
    step = pl.program_id(0)
    group = lax.rem(step, groups)
    halves = columns // LANES
    nx, ny = counts
    a, b = lax.axis_index("px"), lax.axis_index("py")
    targets = (
        (lax.rem(a + nx - 1, nx), b),
        (lax.rem(a + 1, nx), b),
        (a, lax.rem(b + ny - 1, ny)),
        (a, lax.rem(b + 1, ny)),
    )

    @pl.when(step == 0)
    def _():
        barrier = pltpu.get_barrier_semaphore()
        for target in targets:
            pl.semaphore_signal(
                barrier, inc=1, device_id=target, device_id_type=pl.DeviceIdType.MESH
            )
        solved_ref[...] = jnp.zeros_like(solved_ref)
        picked_ref[...] = jnp.zeros_like(picked_ref)
        picked_weight_ref[...] = jnp.ones_like(picked_weight_ref)
        added_ref[...] = jnp.zeros_like(added_ref)
        reader_lane_ref[...] = jnp.full_like(reader_lane_ref, -1)
        for k in range(4):
            reader_lane_ref[:1, k * lanes : k * lanes + shared] = reader_rows_ref[k : k + 1, :]
        pl.semaphore_wait(barrier, 4)

    def remote(source, dest, send_sem, recv_sem, k):
        return pltpu.make_async_remote_copy(
            src_ref=source,
            dst_ref=dest,
            send_sem=send_sem,
            recv_sem=recv_sem,
            device_id=targets[k],
            device_id_type=pl.DeviceIdType.MESH,
        )

    def term_copy(k, g):
        o = OPPOSITE[k]
        return remote(
            term_pay_ref.at[k, g], term_got_ref.at[o, g], term_send.at[k, g], term_recv.at[o, g], k
        )

    def pick_copy(k):
        o = OPPOSITE[k]
        return remote(
            pick_pay_ref.at[k], pick_got_ref.at[o], last_send.at[0, k], last_recv.at[0, o], k
        )

    def weight_copy(part, k):
        o = OPPOSITE[k]
        return remote(
            weight_pay_ref.at[part, k],
            weight_got_ref.at[part, o],
            last_send.at[part + 1, k],
            last_recv.at[part + 1, o],
            k,
        )

    def face_copy(c):
        return pltpu.make_async_copy(
            values_ref.at[c],
            face_ref.at[0, 0, :, pl.ds(c * LANES, LANES)],
            face_sem.at[c],
        )

    @pl.when(step < groups)
    def _():
        count = count_ref[0, 0]
        lane = lax.broadcasted_iota(jnp.int32, (modes, LANES), 1)
        one, zero = jnp.bfloat16(1), jnp.bfloat16(0)
        window_ids = lax.broadcasted_iota(jnp.int32, (windows, modes), 0).astype(jnp.int16)
        weight_cols = weight_ref[...].T
        window_of = (dof_ref[...] // GS).astype(jnp.int16)
        inverse_rows_ref[:, :inner] = inverse_ref[...].astype(jnp.float32).reshape(inner * GS, inner)
        coupling_rows_ref[:, :inner] = (
            coupling_ref[...].astype(jnp.float32).reshape(modes * GS, inner)
        )
        load_rows = load_ref[...].astype(jnp.float32).reshape(inner * GS, columns)
        for c in range(halves):
            load_rows_ref[c] = load_rows[:, c * LANES : (c + 1) * LANES]
        weight_total = jnp.zeros((windows, LANES), jnp.float32)
        for e in range(GS):
            live = group * GS + e < count
            inverse = inverse_rows_ref[pl.ds(e, inner, stride=GS), :][:, :inner].astype(jnp.bfloat16)
            load = jnp.concatenate(
                [load_rows_ref[c, pl.ds(e, inner, stride=GS), :] for c in range(halves)], axis=1
            ).astype(jnp.bfloat16)
            inverse_out_ref[e] = inverse
            load_out_ref[e] = load
            solved = jnp.dot(inverse, load, preferred_element_type=jnp.float32)
            solved = jnp.where(live, solved, 0.0).astype(jnp.bfloat16)
            solved_ref[e, :inner, :] = solved
            col = jnp.where(live, weight_cols[:, e : e + 1], 0.0)
            high = col.astype(jnp.bfloat16).astype(jnp.float32)
            mid = (col - high).astype(jnp.bfloat16).astype(jnp.float32)
            low = col - high - mid
            extra = jnp.where(lane == inner, high, jnp.where(lane == inner + 1, mid, low))
            ext = jnp.where(
                lane < inner, coupling_rows_ref[pl.ds(e, modes, stride=GS), :], extra
            ).astype(jnp.bfloat16)
            onehot = jnp.where(
                window_ids == window_of[e : e + 1, :], one, zero
            )
            spread = jnp.dot(onehot, ext, preferred_element_type=jnp.float32)
            weight_total = weight_total + spread
            spread_ref[group, :, e * LANES : (e + 1) * LANES] = spread.astype(jnp.bfloat16)

        rows = jnp.dot(
            spread_ref[group],
            solved_ref[...].reshape(GS * LANES, columns),
            preferred_element_type=jnp.float32,
        )
        turned_ref[...] = spread_ref[group, own_windows:, :].T
        for k in range(4):
            at = own_windows + starts[k]
            term_pay_ref[k, group] = rows[at : at + span].astype(jnp.bfloat16)
            term_copy(k, group).start()
        wide_lane = lax.broadcasted_iota(jnp.int32, (windows, LANES), 1)
        weight_sum = jnp.sum(jnp.where(wide_lane >= inner, weight_total, 0.0), axis=1, keepdims=True)
        for c in range(halves):
            local_ref[c, pl.ds(group, windows, stride=GS), :] = rows[:, c * LANES : (c + 1) * LANES]
        local_weight_ref[pl.ds(group, windows, stride=GS), :] = jnp.broadcast_to(
            weight_sum, (windows, LANES)
        )

    @pl.when(step == groups - 1)
    def _():
        for k in range(4):
            start = owned + k * shared
            weight_pay_ref[0, k] = local_weight_ref[start : start + lanes, :].T[:8]
            weight_copy(0, k).start()

        def subtract(chunk, carry):
            at = pl.ds(pl.multiple_of(chunk * LANES, LANES), LANES)
            for c in range(halves):
                values_ref[c, at, :] = (
                    edge_ref[at, c * LANES : (c + 1) * LANES].astype(jnp.float32)
                    - local_ref[c, at, :]
                )
            own = jnp.broadcast_to(owner_ref[:, at], (LANES, LANES)).T
            pre_weight_ref[at, :] = own + local_weight_ref[at, :]
            return carry

        lax.fori_loop(0, owned // LANES, subtract, 0, unroll=4)

        for pair in ((0, 1), (2, 3)):

            def pick(s, carry):
                loaded = []
                for k in pair:
                    r = readers_ref[k, s]
                    loaded.append(
                        (
                            [values_ref[c, pl.ds(r, 1), :] for c in range(halves)],
                            pre_weight_ref[pl.ds(r, 1), :],
                        )
                    )
                for k, (values, weight) in zip(pair, loaded):
                    for c in range(halves):
                        picked_ref[k, c, pl.ds(s, 1), :] = values[c]
                    picked_weight_ref[k, pl.ds(s, 1), :] = weight
                return carry

            lax.fori_loop(0, shared, pick, 0, unroll=6)
            for k in pair:
                for c in range(halves):
                    pick_pay_ref[k, :, c * LANES : (c + 1) * LANES] = picked_ref[k, c].astype(
                        jnp.bfloat16
                    )
                pick_copy(k).start()
                weight_pay_ref[1, k] = picked_weight_ref[k].T[:8]
                weight_copy(1, k).start()

        for k in range(4):

            def settle(g, carry):
                term_copy(k, g).wait()
                return carry

            lax.fori_loop(0, groups, settle, 0)
            weight_copy(0, k).wait()
        for k in range(4):
            for g in range(groups):
                piece = term_got_ref[k, g].astype(jnp.float32)
                for c in range(halves):
                    incoming_ref[k, c, pl.ds(g, span, stride=GS), :] = piece[
                        :, c * LANES : (c + 1) * LANES
                    ]
            shift = shifts[OPPOSITE[k]]
            before = picked_weight_ref[k, :pad, :]
            after = 1.0 / (before + weight_got_ref[0, k].T[:pad, 0:1])
            before = 1.0 / before
            real = lax.broadcasted_iota(jnp.int32, (pad, LANES), 0) < shared
            for c in range(halves):
                picked = picked_ref[k, c]
                incoming = incoming_ref[k, c, shift : shift + pad, :]
                change = (picked - incoming) * after - picked * before
                added_ref[k * lanes : k * lanes + pad, c * LANES : (c + 1) * LANES] = jnp.where(
                    real, change, 0.0
                ).astype(jnp.bfloat16)

        row_ids = lax.broadcasted_iota(jnp.int32, (2 * LANES, 4 * lanes), 0).astype(jnp.int16)
        one, zero = jnp.bfloat16(1), jnp.bfloat16(0)

        def finish(chunk, carry):
            at = pl.ds(pl.multiple_of(chunk * 2 * LANES, 2 * LANES), 2 * LANES)
            wanted = (reader_lane_ref[:1, :] - chunk * 2 * LANES).astype(jnp.int16)
            onehot = jnp.where(row_ids == wanted, one, zero)
            added = jnp.dot(onehot, added_ref[...], preferred_element_type=jnp.float32)
            scale = 1.0 / pre_weight_ref[at, :]
            for c in range(halves):
                values_ref[c, at, :] = (
                    values_ref[c, at, :] * scale + added[:, c * LANES : (c + 1) * LANES]
                )
            return carry

        lax.fori_loop(0, owned // (2 * LANES), finish, 0)
        for c in range(halves):
            face_copy(c).start()

    @pl.when(step >= groups)
    def _():
        table = jnp.concatenate(
            [values_ref[c, pl.ds(group, own_windows, stride=GS), :] for c in range(halves)], axis=1
        )
        part_ref[...] = jnp.dot(
            table.T.astype(jnp.bfloat16),
            spread_ref[group, :own_windows, :],
            preferred_element_type=jnp.float32,
        ).T

    @pl.when(step == 2 * groups - 1)
    def _():
        for k in range(4):
            pick_copy(k).wait()
            weight_copy(1, k).wait()
        theirs_ref[...] = jnp.zeros_like(theirs_ref)
        for k in range(4):
            weights = weight_got_ref[1, k].T
            start = owned + k * shared
            scale = 1.0 / (local_weight_ref[start : start + pad, :] + weights[:pad, 0:1])
            for c in range(halves):
                theirs = (
                    pick_got_ref[k, :, c * LANES : (c + 1) * LANES].astype(jnp.float32)
                    - local_ref[c, start : start + pad, :]
                ) * scale
                theirs_ref[c, k * shared : (k + 1) * shared, :] = theirs[:shared]
        for g in range(groups):
            for c in range(halves):
                shared_ref[g, :, c * LANES : (c + 1) * LANES] = theirs_ref[
                    c, pl.ds(g, windows - own_windows, stride=GS), :
                ].astype(jnp.bfloat16)
        for c in range(halves):
            face_copy(c).wait()


def recover_kernel(
    sizes,
    count_ref,
    face_in_ref,
    turned_ref,
    shared_ref,
    part_ref,
    inverse_ref,
    load_ref,
    face_ref,
    out_ref,
    out_rows_ref,
):
    slots, modes, inner, columns, owned, shared, windows, pad, lanes, span = sizes
    group = pl.program_id(0)
    halves = columns // LANES
    groups = slots // GS

    face_ref[...] = face_in_ref[...]
    pulled = part_ref[...] + jnp.dot(
        turned_ref[...], shared_ref[group], preferred_element_type=jnp.float32
    )
    count = count_ref[0, 0]
    for e in range(GS):
        live = group * GS + e < count
        reduced = (
            load_ref[e].astype(jnp.float32) - pulled[e * LANES : e * LANES + inner]
        ).astype(jnp.bfloat16)
        result = jnp.dot(inverse_ref[e], reduced, preferred_element_type=jnp.float32)
        result = jnp.where(live, result, 0.0)
        for c in range(halves):
            out_rows_ref[c, pl.ds(e, inner, stride=GS), :] = result[:, c * LANES : (c + 1) * LANES]
    out_ref[...] = (
        jnp.concatenate([out_rows_ref[c] for c in range(halves)], axis=1)
        .reshape(inner, GS, columns)
        .astype(jnp.bfloat16)
    )


def per_device(
    counts,
    coupling,
    interior_inverse,
    interior_load,
    boundary_load,
    owner_weight,
    elem_weight,
    elem_dof,
    reader_rows,
    elem_count,
):
    slots, modes, inner = coupling.shape[2:]
    columns = interior_load.shape[-1]
    owned = boundary_load.shape[2]
    shared = reader_rows.shape[3]
    groups = slots // GS
    halves = columns // LANES
    windows = round_up((owned + 4 * shared) // GS, 16)
    pad = round_up(shared, 16)
    span = round_up(shared // GS + 2, 16)
    lanes = round_up(shared, LANES)
    own_windows = owned // GS
    shared_windows = windows - own_windows
    sizes = (slots, modes, inner, columns, owned, shared, windows, pad, lanes, span)
    f32, bf16 = jnp.float32, jnp.bfloat16
    smem = pl.BlockSpec(memory_space=pltpu.SMEM)
    vmem = pl.BlockSpec(memory_space=pltpu.VMEM)
    anyplace = pl.BlockSpec(memory_space=pl.ANY)

    def at_first(g):
        return jnp.minimum(g, groups - 1)

    def by_group(*tail):
        zeros = (0,) * len(tail)
        return pl.BlockSpec((None, None, GS) + tail, lambda g: (0, 0, at_first(g)) + zeros)

    def by_mode(rows, width):
        return pl.BlockSpec(
            (None, None, rows, GS, width), lambda g: (0, 0, 0, at_first(g), 0)
        )

    def by_slot(rows, width):
        return pl.BlockSpec((GS, rows, width), lambda g: (at_first(g), 0, 0))

    def modes_first(array):
        return jnp.swapaxes(array, 2, 3)

    turned_spec = pl.BlockSpec(
        (None, GS * LANES, shared_windows), lambda g: (at_first(g), 0, 0)
    )
    face_spec = pl.BlockSpec((None, None, owned // groups, columns), lambda g: (0, 0, g, 0))
    part_block = (None, GS * LANES, columns)
    readers = reader_rows[0, 0]
    params = dict(vmem_limit_bytes=VMEM_BYTES, dimension_semantics=("arbitrary",))
    shape = jax.ShapeDtypeStruct
    turned, inverse_rows, load_rows, face_mid, part, shared_values = pl.pallas_call(
        functools.partial(condense_kernel, sizes, counts),
        grid=(2 * groups,),
        in_specs=[
            smem,
            smem,
            by_mode(inner, inner),
            by_mode(inner, columns),
            by_mode(modes, inner),
            by_group(modes),
            by_group(modes),
            vmem,
            vmem,
            vmem,
        ],
        out_specs=[
            turned_spec,
            by_slot(inner, inner),
            by_slot(inner, columns),
            anyplace,
            pl.BlockSpec(part_block, lambda g: (jnp.maximum(g - groups, 0), 0, 0)),
            vmem,
        ],
        out_shape=[
            shape((groups, GS * LANES, shared_windows), bf16),
            shape((slots, inner, inner), bf16),
            shape((slots, inner, columns), bf16),
            shape((1, 1, owned, columns), f32),
            shape((groups, GS * LANES, columns), f32),
            shape((groups, shared_windows, columns), bf16),
        ],
        scratch_shapes=[
            pltpu.VMEM((halves, owned, LANES), f32),
            pltpu.VMEM((groups, windows, GS * LANES), bf16),
            pltpu.VMEM((halves, windows * GS, LANES), f32),
            pltpu.VMEM((windows * GS + LANES, LANES), f32),
            pltpu.VMEM((owned, LANES), f32),
            pltpu.VMEM((GS, LANES, columns), bf16),
            pltpu.VMEM((inner * GS, LANES), f32),
            pltpu.VMEM((halves, inner * GS, LANES), f32),
            pltpu.VMEM((modes * GS, LANES), f32),
            pltpu.VMEM((4, halves, pad, LANES), f32),
            pltpu.VMEM((4, lanes, LANES), f32),
            pltpu.VMEM((4, halves, span * GS, LANES), f32),
            pltpu.VMEM((4 * lanes, columns), bf16),
            pltpu.VMEM((8, 4 * lanes), jnp.int32),
            pltpu.VMEM((halves, shared_windows * GS, LANES), f32),
            pltpu.VMEM((4, groups, span, columns), bf16),
            pltpu.VMEM((4, groups, span, columns), bf16),
            pltpu.VMEM((4, pad, columns), bf16),
            pltpu.VMEM((4, pad, columns), bf16),
            pltpu.VMEM((2, 4, 8, lanes), f32),
            pltpu.VMEM((2, 4, 8, lanes), f32),
            pltpu.SemaphoreType.DMA((4, groups)),
            pltpu.SemaphoreType.DMA((4, groups)),
            pltpu.SemaphoreType.DMA((3, 4)),
            pltpu.SemaphoreType.DMA((3, 4)),
            pltpu.SemaphoreType.DMA((halves,)),
        ],
        compiler_params=pltpu.CompilerParams(
            collective_id=0, has_side_effects=True, **params
        ),
        name="condense",
    )(
        elem_count,
        readers,
        modes_first(interior_inverse),
        modes_first(interior_load),
        modes_first(coupling),
        elem_weight,
        elem_dof,
        boundary_load[0, 0],
        owner_weight[0],
        readers,
    )
    face, interior = pl.pallas_call(
        functools.partial(recover_kernel, sizes),
        grid=(groups,),
        in_specs=[
            smem,
            face_spec,
            turned_spec,
            vmem,
            pl.BlockSpec(part_block, lambda g: (g, 0, 0)),
            by_slot(inner, inner),
            by_slot(inner, columns),
        ],
        out_specs=[face_spec, by_mode(inner, columns)],
        out_shape=[
            shape((1, 1, owned, columns), f32),
            shape((1, 1, inner, slots, columns), bf16),
        ],
        scratch_shapes=[
            pltpu.VMEM((halves, inner * GS, LANES), f32),
        ],
        compiler_params=pltpu.CompilerParams(**params),
        name="recover",
    )(elem_count, face_mid, turned, shared_values, part, inverse_rows, load_rows)
    return face, modes_first(interior)


def solution(mesh):
    in_specs = (
        P("px", "py", None, None, None),
        P("px", "py", None, None, None),
        P("px", "py", None, None, None),
        P("px", "py", None, None),
        P("px", "py", None),
        P("px", "py", None, None),
        P("px", "py", None, None),
        P("px", "py", None, None),
        P("px", "py"),
    )
    out_specs = (P("px", "py", None, None), P("px", "py", None, None, None))
    counts = (mesh.shape["px"], mesh.shape["py"])
    return jax.shard_map(
        functools.partial(per_device, counts),
        mesh=mesh,
        in_specs=in_specs,
        out_specs=out_specs,
        check_vma=False,
    )
```

```python
import functools

import jax
import jax.numpy as jnp
from jax import lax
from jax.experimental import pallas as pl
from jax.experimental.pallas import tpu as pltpu
from jax.sharding import PartitionSpec as P

GS = 8
LANES = 128
VMEM_BYTES = 58 * 2**20
OPPOSITE = (1, 0, 3, 2)


def round_up(value, unit):
    return (value + unit - 1) // unit * unit


def condense_kernel(
    sizes,
    counts,
    count_ref,
    readers_ref,
    inverse_ref,
    load_ref,
    coupling_ref,
    weight_ref,
    dof_ref,
    edge_ref,
    owner_ref,
    reader_rows_ref,
    face_ref,
    out_ref,
    values_ref,
    spread_ref,
    inverse_all_ref,
    load_all_ref,
    out_rows_ref,
    local_ref,
    local_weight_ref,
    pre_weight_ref,
    solved_ref,
    inverse_rows_ref,
    load_rows_ref,
    coupling_rows_ref,
    picked_ref,
    picked_weight_ref,
    incoming_ref,
    added_ref,
    reader_lane_ref,
    theirs_ref,
    term_pay_ref,
    term_got_ref,
    pick_pay_ref,
    pick_got_ref,
    weight_pay_ref,
    weight_got_ref,
    term_send,
    term_recv,
    last_send,
    last_recv,
    face_sem,
):
    slots, modes, inner, columns, owned, shared, windows, pad, lanes, span = sizes
    groups = slots // GS
    own_windows = owned // GS
    starts = [min(k * shared // GS, windows - own_windows - span) for k in range(4)]
    shifts = [k * shared - GS * starts[k] for k in range(4)]
    step = pl.program_id(0)
    group = lax.rem(step, groups)
    halves = columns // LANES
    nx, ny = counts
    a, b = lax.axis_index("px"), lax.axis_index("py")
    targets = (
        (lax.rem(a + nx - 1, nx), b),
        (lax.rem(a + 1, nx), b),
        (a, lax.rem(b + ny - 1, ny)),
        (a, lax.rem(b + 1, ny)),
    )

    @pl.when(step == 0)
    def _():
        barrier = pltpu.get_barrier_semaphore()
        for target in targets:
            pl.semaphore_signal(
                barrier, inc=1, device_id=target, device_id_type=pl.DeviceIdType.MESH
            )
        solved_ref[...] = jnp.zeros_like(solved_ref)
        picked_ref[...] = jnp.zeros_like(picked_ref)
        picked_weight_ref[...] = jnp.ones_like(picked_weight_ref)
        added_ref[...] = jnp.zeros_like(added_ref)
        reader_lane_ref[...] = jnp.full_like(reader_lane_ref, -1)
        for k in range(4):
            reader_lane_ref[:1, k * lanes : k * lanes + shared] = reader_rows_ref[k : k + 1, :]
        pl.semaphore_wait(barrier, 4)

    def remote(source, dest, send_sem, recv_sem, k):
        return pltpu.make_async_remote_copy(
            src_ref=source,
            dst_ref=dest,
            send_sem=send_sem,
            recv_sem=recv_sem,
            device_id=targets[k],
            device_id_type=pl.DeviceIdType.MESH,
        )

    def term_copy(k, g):
        o = OPPOSITE[k]
        return remote(
            term_pay_ref.at[k, g], term_got_ref.at[o, g], term_send.at[k, g], term_recv.at[o, g], k
        )

    def pick_copy(k):
        o = OPPOSITE[k]
        return remote(
            pick_pay_ref.at[k], pick_got_ref.at[o], last_send.at[0, k], last_recv.at[0, o], k
        )

    def weight_copy(part, k):
        o = OPPOSITE[k]
        return remote(
            weight_pay_ref.at[part, k],
            weight_got_ref.at[part, o],
            last_send.at[part + 1, k],
            last_recv.at[part + 1, o],
            k,
        )

    def face_copy(c):
        return pltpu.make_async_copy(
            values_ref.at[c],
            face_ref.at[0, 0, :, pl.ds(c * LANES, LANES)],
            face_sem.at[c],
        )

    @pl.when(step < groups)
    def _():
        count = count_ref[0, 0]
        lane = lax.broadcasted_iota(jnp.int32, (modes, LANES), 1)
        one, zero = jnp.bfloat16(1), jnp.bfloat16(0)
        window_ids = lax.broadcasted_iota(jnp.int32, (windows, modes), 0).astype(jnp.int16)
        weight_cols = weight_ref[...].T
        window_of = (dof_ref[...] // GS).astype(jnp.int16)
        inverse_rows_ref[:, :inner] = inverse_ref[...].astype(jnp.float32).reshape(inner * GS, inner)
        coupling_rows_ref[:, :inner] = (
            coupling_ref[...].astype(jnp.float32).reshape(modes * GS, inner)
        )
        load_rows = load_ref[...].astype(jnp.float32).reshape(inner * GS, columns)
        for c in range(halves):
            load_rows_ref[c] = load_rows[:, c * LANES : (c + 1) * LANES]
        weight_total = jnp.zeros((windows, LANES), jnp.float32)
        for e in range(GS):
            live = group * GS + e < count
            inverse = inverse_rows_ref[pl.ds(e, inner, stride=GS), :][:, :inner].astype(jnp.bfloat16)
            load = jnp.concatenate(
                [load_rows_ref[c, pl.ds(e, inner, stride=GS), :] for c in range(halves)], axis=1
            ).astype(jnp.bfloat16)
            inverse_all_ref[group * GS + e] = inverse
            load_all_ref[group * GS + e] = load
            solved = jnp.dot(inverse, load, preferred_element_type=jnp.float32)
            solved = jnp.where(live, solved, 0.0).astype(jnp.bfloat16)
            solved_ref[e, :inner, :] = solved
            col = jnp.where(live, weight_cols[:, e : e + 1], 0.0)
            high = col.astype(jnp.bfloat16).astype(jnp.float32)
            mid = (col - high).astype(jnp.bfloat16).astype(jnp.float32)
            low = col - high - mid
            extra = jnp.where(lane == inner, high, jnp.where(lane == inner + 1, mid, low))
            ext = jnp.where(
                lane < inner, coupling_rows_ref[pl.ds(e, modes, stride=GS), :], extra
            ).astype(jnp.bfloat16)
            onehot = jnp.where(
                window_ids == window_of[e : e + 1, :], one, zero
            )
            spread = jnp.dot(onehot, ext, preferred_element_type=jnp.float32)
            weight_total = weight_total + spread
            spread_ref[group, :, e * LANES : (e + 1) * LANES] = spread.astype(jnp.bfloat16)

        rows = jnp.dot(
            spread_ref[group],
            solved_ref[...].reshape(GS * LANES, columns),
            preferred_element_type=jnp.float32,
        )
        for k in range(4):
            at = own_windows + starts[k]
            term_pay_ref[k, group] = rows[at : at + span].astype(jnp.bfloat16)
            term_copy(k, group).start()
        wide_lane = lax.broadcasted_iota(jnp.int32, (windows, LANES), 1)
        weight_sum = jnp.sum(jnp.where(wide_lane >= inner, weight_total, 0.0), axis=1, keepdims=True)
        for c in range(halves):
            local_ref[c, pl.ds(group, windows, stride=GS), :] = rows[:, c * LANES : (c + 1) * LANES]
        local_weight_ref[pl.ds(group, windows, stride=GS), :] = jnp.broadcast_to(
            weight_sum, (windows, LANES)
        )

    @pl.when(step == groups - 1)
    def _():
        for k in range(4):
            start = owned + k * shared
            weight_pay_ref[0, k] = local_weight_ref[start : start + lanes, :].T[:8]
            weight_copy(0, k).start()

        def subtract(chunk, carry):
            at = pl.ds(pl.multiple_of(chunk * LANES, LANES), LANES)
            for c in range(halves):
                values_ref[c, at, :] = (
                    edge_ref[at, c * LANES : (c + 1) * LANES].astype(jnp.float32)
                    - local_ref[c, at, :]
                )
            own = jnp.broadcast_to(owner_ref[:, at], (LANES, LANES)).T
            pre_weight_ref[at, :] = own + local_weight_ref[at, :]
            return carry

        lax.fori_loop(0, owned // LANES, subtract, 0, unroll=4)

        for pair in ((0, 1), (2, 3)):

            def pick(s, carry):
                loaded = []
                for k in pair:
                    r = readers_ref[k, s]
                    loaded.append(
                        (
                            [values_ref[c, pl.ds(r, 1), :] for c in range(halves)],
                            pre_weight_ref[pl.ds(r, 1), :],
                        )
                    )
                for k, (values, weight) in zip(pair, loaded):
                    for c in range(halves):
                        picked_ref[k, c, pl.ds(s, 1), :] = values[c]
                    picked_weight_ref[k, pl.ds(s, 1), :] = weight
                return carry

            lax.fori_loop(0, shared, pick, 0, unroll=6)
            for k in pair:
                for c in range(halves):
                    pick_pay_ref[k, :, c * LANES : (c + 1) * LANES] = picked_ref[k, c].astype(
                        jnp.bfloat16
                    )
                pick_copy(k).start()
                weight_pay_ref[1, k] = picked_weight_ref[k].T[:8]
                weight_copy(1, k).start()

        for k in range(4):

            def settle(g, carry):
                term_copy(k, g).wait()
                return carry

            lax.fori_loop(0, groups, settle, 0)
            weight_copy(0, k).wait()
        for k in range(4):
            for g in range(groups):
                piece = term_got_ref[k, g].astype(jnp.float32)
                for c in range(halves):
                    incoming_ref[k, c, pl.ds(g, span, stride=GS), :] = piece[
                        :, c * LANES : (c + 1) * LANES
                    ]
            shift = shifts[OPPOSITE[k]]
            before = picked_weight_ref[k, :pad, :]
            after = 1.0 / (before + weight_got_ref[0, k].T[:pad, 0:1])
            before = 1.0 / before
            real = lax.broadcasted_iota(jnp.int32, (pad, LANES), 0) < shared
            for c in range(halves):
                picked = picked_ref[k, c]
                incoming = incoming_ref[k, c, shift : shift + pad, :]
                change = (picked - incoming) * after - picked * before
                added_ref[k * lanes : k * lanes + pad, c * LANES : (c + 1) * LANES] = jnp.where(
                    real, change, 0.0
                ).astype(jnp.bfloat16)

        row_ids = lax.broadcasted_iota(jnp.int32, (2 * LANES, 4 * lanes), 0).astype(jnp.int16)
        one, zero = jnp.bfloat16(1), jnp.bfloat16(0)

        def finish(chunk, carry):
            at = pl.ds(pl.multiple_of(chunk * 2 * LANES, 2 * LANES), 2 * LANES)
            wanted = (reader_lane_ref[:1, :] - chunk * 2 * LANES).astype(jnp.int16)
            onehot = jnp.where(row_ids == wanted, one, zero)
            added = jnp.dot(onehot, added_ref[...], preferred_element_type=jnp.float32)
            scale = 1.0 / pre_weight_ref[at, :]
            for c in range(halves):
                values_ref[c, at, :] = (
                    values_ref[c, at, :] * scale + added[:, c * LANES : (c + 1) * LANES]
                )
            return carry

        lax.fori_loop(0, owned // (2 * LANES), finish, 0)
        for c in range(halves):
            face_copy(c).start()

    @pl.when(step == groups)
    def _():
        for k in (2, 3, 0, 1):
            pick_copy(k).wait()
            weight_copy(1, k).wait()
        theirs_ref[...] = jnp.zeros_like(theirs_ref)
        for k in range(4):
            weights = weight_got_ref[1, k].T
            start = owned + k * shared
            scale = 1.0 / (local_weight_ref[start : start + pad, :] + weights[:pad, 0:1])
            for c in range(halves):
                theirs = (
                    pick_got_ref[k, :, c * LANES : (c + 1) * LANES].astype(jnp.float32)
                    - local_ref[c, start : start + pad, :]
                ) * scale
                theirs_ref[c, k * shared : (k + 1) * shared, :] = theirs[:shared]

    @pl.when(step >= groups)
    def _():
        table = jnp.concatenate(
            [
                jnp.concatenate(
                    [
                        values_ref[c, pl.ds(group, own_windows, stride=GS), :],
                        theirs_ref[c, pl.ds(group, windows - own_windows, stride=GS), :],
                    ],
                    axis=0,
                )
                for c in range(halves)
            ],
            axis=1,
        )
        pulled = jnp.dot(
            table.T.astype(jnp.bfloat16), spread_ref[group], preferred_element_type=jnp.float32
        )
        for e in range(GS):
            slot = group * GS + e
            part = pulled[:, e * LANES : (e + 1) * LANES].T[:inner]
            reduced = (load_all_ref[slot].astype(jnp.float32) - part).astype(jnp.bfloat16)
            result = jnp.dot(
                inverse_all_ref[slot], reduced, preferred_element_type=jnp.float32
            )
            result = jnp.where(slot < count_ref[0, 0], result, 0.0)
            for c in range(halves):
                out_rows_ref[c, pl.ds(e, inner, stride=GS), :] = result[
                    :, c * LANES : (c + 1) * LANES
                ]
        out_ref[...] = (
            jnp.concatenate([out_rows_ref[c] for c in range(halves)], axis=1)
            .reshape(inner, GS, columns)
            .astype(jnp.bfloat16)
        )

    @pl.when(step == 2 * groups - 1)
    def _():
        for c in range(halves):
            face_copy(c).wait()


def per_device(
    counts,
    coupling,
    interior_inverse,
    interior_load,
    boundary_load,
    owner_weight,
    elem_weight,
    elem_dof,
    reader_rows,
    elem_count,
):
    slots, modes, inner = coupling.shape[2:]
    columns = interior_load.shape[-1]
    owned = boundary_load.shape[2]
    shared = reader_rows.shape[3]
    groups = slots // GS
    halves = columns // LANES
    windows = round_up((owned + 4 * shared) // GS, 16)
    pad = round_up(shared, 16)
    span = round_up(shared // GS + 2, 16)
    lanes = round_up(shared, LANES)
    own_windows = owned // GS
    shared_windows = windows - own_windows
    sizes = (slots, modes, inner, columns, owned, shared, windows, pad, lanes, span)
    f32, bf16 = jnp.float32, jnp.bfloat16
    smem = pl.BlockSpec(memory_space=pltpu.SMEM)
    vmem = pl.BlockSpec(memory_space=pltpu.VMEM)
    anyplace = pl.BlockSpec(memory_space=pl.ANY)

    def at_first(g):
        return jnp.minimum(g, groups - 1)

    def by_group(*tail):
        zeros = (0,) * len(tail)
        return pl.BlockSpec((None, None, GS) + tail, lambda g: (0, 0, at_first(g)) + zeros)

    def by_mode(rows, width):
        return pl.BlockSpec(
            (None, None, rows, GS, width), lambda g: (0, 0, 0, at_first(g), 0)
        )

    def modes_first(array):
        return jnp.swapaxes(array, 2, 3)

    readers = reader_rows[0, 0]
    params = dict(vmem_limit_bytes=VMEM_BYTES, dimension_semantics=("arbitrary",))
    shape = jax.ShapeDtypeStruct
    face, interior = pl.pallas_call(
        functools.partial(condense_kernel, sizes, counts),
        grid=(2 * groups,),
        in_specs=[
            smem,
            smem,
            by_mode(inner, inner),
            by_mode(inner, columns),
            by_mode(modes, inner),
            by_group(modes),
            by_group(modes),
            vmem,
            vmem,
            vmem,
        ],
        out_specs=[
            anyplace,
            pl.BlockSpec(
                (None, None, inner, GS, columns),
                lambda g: (0, 0, 0, jnp.maximum(g - groups, 0), 0),
            ),
        ],
        out_shape=[
            shape((1, 1, owned, columns), f32),
            shape((1, 1, inner, slots, columns), bf16),
        ],
        scratch_shapes=[
            pltpu.VMEM((halves, owned, LANES), f32),
            pltpu.VMEM((groups, windows, GS * LANES), bf16),
            pltpu.VMEM((slots, inner, inner), bf16),
            pltpu.VMEM((slots, inner, columns), bf16),
            pltpu.VMEM((halves, inner * GS, LANES), f32),
            pltpu.VMEM((halves, windows * GS, LANES), f32),
            pltpu.VMEM((windows * GS + LANES, LANES), f32),
            pltpu.VMEM((owned, LANES), f32),
            pltpu.VMEM((GS, LANES, columns), bf16),
            pltpu.VMEM((inner * GS, LANES), f32),
            pltpu.VMEM((halves, inner * GS, LANES), f32),
            pltpu.VMEM((modes * GS, LANES), f32),
            pltpu.VMEM((4, halves, pad, LANES), f32),
            pltpu.VMEM((4, lanes, LANES), f32),
            pltpu.VMEM((4, halves, span * GS, LANES), f32),
            pltpu.VMEM((4 * lanes, columns), bf16),
            pltpu.VMEM((8, 4 * lanes), jnp.int32),
            pltpu.VMEM((halves, shared_windows * GS, LANES), f32),
            pltpu.VMEM((4, groups, span, columns), bf16),
            pltpu.VMEM((4, groups, span, columns), bf16),
            pltpu.VMEM((4, pad, columns), bf16),
            pltpu.VMEM((4, pad, columns), bf16),
            pltpu.VMEM((2, 4, 8, lanes), f32),
            pltpu.VMEM((2, 4, 8, lanes), f32),
            pltpu.SemaphoreType.DMA((4, groups)),
            pltpu.SemaphoreType.DMA((4, groups)),
            pltpu.SemaphoreType.DMA((3, 4)),
            pltpu.SemaphoreType.DMA((3, 4)),
            pltpu.SemaphoreType.DMA((halves,)),
        ],
        compiler_params=pltpu.CompilerParams(
            collective_id=0, has_side_effects=True, **params
        ),
        name="condense_recover",
    )(
        elem_count,
        readers,
        modes_first(interior_inverse),
        modes_first(interior_load),
        modes_first(coupling),
        elem_weight,
        elem_dof,
        boundary_load[0, 0],
        owner_weight[0],
        readers,
    )
    return face, modes_first(interior)


def solution(mesh):
    in_specs = (
        P("px", "py", None, None, None),
        P("px", "py", None, None, None),
        P("px", "py", None, None, None),
        P("px", "py", None, None),
        P("px", "py", None),
        P("px", "py", None, None),
        P("px", "py", None, None),
        P("px", "py", None, None),
        P("px", "py"),
    )
    out_specs = (P("px", "py", None, None), P("px", "py", None, None, None))
    counts = (mesh.shape["px"], mesh.shape["py"])
    return jax.shard_map(
        functools.partial(per_device, counts),
        mesh=mesh,
        in_specs=in_specs,
        out_specs=out_specs,
        check_vma=False,
    )
```

```python
import functools

import jax
import jax.numpy as jnp
from jax import lax
from jax.experimental import pallas as pl
from jax.experimental.pallas import tpu as pltpu
from jax.sharding import PartitionSpec as P

GS = 8
LANES = 128
VMEM_BYTES = 58 * 2**20
OPPOSITE = (1, 0, 3, 2)


def round_up(value, unit):
    return (value + unit - 1) // unit * unit


def condense_kernel(
    sizes,
    counts,
    count_ref,
    readers_ref,
    inverse_ref,
    load_ref,
    coupling_ref,
    weight_ref,
    dof_ref,
    edge_ref,
    owner_ref,
    reader_rows_ref,
    face_ref,
    out_ref,
    values_ref,
    spread_ref,
    inverse_all_ref,
    load_all_ref,
    out_rows_ref,
    local_ref,
    local_weight_ref,
    pre_weight_ref,
    solved_ref,
    inverse_rows_ref,
    load_rows_ref,
    coupling_rows_ref,
    picked_ref,
    picked_weight_ref,
    incoming_ref,
    added_ref,
    reader_lane_ref,
    theirs_ref,
    term_pay_ref,
    term_got_ref,
    pick_pay_ref,
    pick_got_ref,
    weight_pay_ref,
    weight_got_ref,
    term_send,
    term_recv,
    last_send,
    last_recv,
    face_sem,
):
    slots, modes, inner, columns, owned, shared, windows, pad, lanes, span = sizes
    groups = slots // GS
    own_windows = owned // GS
    starts = [min(k * shared // GS, windows - own_windows - span) for k in range(4)]
    shifts = [k * shared - GS * starts[k] for k in range(4)]
    step = pl.program_id(0)
    group = lax.rem(step, groups)
    halves = columns // LANES
    nx, ny = counts
    a, b = lax.axis_index("px"), lax.axis_index("py")
    targets = (
        (lax.rem(a + nx - 1, nx), b),
        (lax.rem(a + 1, nx), b),
        (a, lax.rem(b + ny - 1, ny)),
        (a, lax.rem(b + 1, ny)),
    )

    @pl.when(step == 0)
    def _():
        barrier = pltpu.get_barrier_semaphore()
        for target in targets:
            pl.semaphore_signal(
                barrier, inc=1, device_id=target, device_id_type=pl.DeviceIdType.MESH
            )
        solved_ref[...] = jnp.zeros_like(solved_ref)
        picked_ref[...] = jnp.zeros_like(picked_ref)
        picked_weight_ref[...] = jnp.ones_like(picked_weight_ref)
        added_ref[...] = jnp.zeros_like(added_ref)
        reader_lane_ref[...] = jnp.full_like(reader_lane_ref, -1)
        for k in range(4):
            reader_lane_ref[:1, k * lanes : k * lanes + shared] = reader_rows_ref[k : k + 1, :]
        pl.semaphore_wait(barrier, 4)

    def remote(source, dest, send_sem, recv_sem, k):
        return pltpu.make_async_remote_copy(
            src_ref=source,
            dst_ref=dest,
            send_sem=send_sem,
            recv_sem=recv_sem,
            device_id=targets[k],
            device_id_type=pl.DeviceIdType.MESH,
        )

    def term_copy(k, g):
        o = OPPOSITE[k]
        return remote(
            term_pay_ref.at[k, g], term_got_ref.at[o, g], term_send.at[k, g], term_recv.at[o, g], k
        )

    def pick_copy(k):
        o = OPPOSITE[k]
        return remote(
            pick_pay_ref.at[k], pick_got_ref.at[o], last_send.at[0, k], last_recv.at[0, o], k
        )

    def weight_copy(part, k):
        o = OPPOSITE[k]
        return remote(
            weight_pay_ref.at[part, k],
            weight_got_ref.at[part, o],
            last_send.at[part + 1, k],
            last_recv.at[part + 1, o],
            k,
        )

    def face_copy(c):
        return pltpu.make_async_copy(
            values_ref.at[c],
            face_ref.at[0, 0, :, pl.ds(c * LANES, LANES)],
            face_sem.at[c],
        )

    @pl.when(step < groups)
    def _():
        count = count_ref[0, 0]
        lane = lax.broadcasted_iota(jnp.int32, (modes, LANES), 1)
        one, zero = jnp.bfloat16(1), jnp.bfloat16(0)
        window_ids = lax.broadcasted_iota(jnp.int32, (windows, modes), 0).astype(jnp.int16)
        weight_cols = weight_ref[...].T
        window_of = (dof_ref[...] // GS).astype(jnp.int16)
        inverse_rows_ref[:, :inner] = inverse_ref[...].astype(jnp.float32).reshape(inner * GS, inner)
        coupling_rows_ref[:, :inner] = (
            coupling_ref[...].astype(jnp.float32).reshape(modes * GS, inner)
        )
        load_rows = load_ref[...].astype(jnp.float32).reshape(inner * GS, columns)
        for c in range(halves):
            load_rows_ref[c] = load_rows[:, c * LANES : (c + 1) * LANES]
        weight_total = jnp.zeros((windows, LANES), jnp.float32)
        for e in range(GS):
            live = group * GS + e < count
            inverse = inverse_rows_ref[pl.ds(e, inner, stride=GS), :][:, :inner].astype(jnp.bfloat16)
            load = jnp.concatenate(
                [load_rows_ref[c, pl.ds(e, inner, stride=GS), :] for c in range(halves)], axis=1
            ).astype(jnp.bfloat16)
            inverse_all_ref[group * GS + e] = inverse
            load_all_ref[group * GS + e] = load
            solved = jnp.dot(inverse, load, preferred_element_type=jnp.float32)
            solved = jnp.where(live, solved, 0.0).astype(jnp.bfloat16)
            solved_ref[e, :inner, :] = solved
            col = jnp.where(live, weight_cols[:, e : e + 1], 0.0)
            high = col.astype(jnp.bfloat16).astype(jnp.float32)
            mid = (col - high).astype(jnp.bfloat16).astype(jnp.float32)
            low = col - high - mid
            extra = jnp.where(lane == inner, high, jnp.where(lane == inner + 1, mid, low))
            ext = jnp.where(
                lane < inner, coupling_rows_ref[pl.ds(e, modes, stride=GS), :], extra
            ).astype(jnp.bfloat16)
            onehot = jnp.where(
                window_ids == window_of[e : e + 1, :], one, zero
            )
            spread = jnp.dot(onehot, ext, preferred_element_type=jnp.float32)
            weight_total = weight_total + spread
            spread_ref[group, :, e * LANES : (e + 1) * LANES] = spread.astype(jnp.bfloat16)

        rows = jnp.dot(
            spread_ref[group],
            solved_ref[...].reshape(GS * LANES, columns),
            preferred_element_type=jnp.float32,
        )
        for k in range(4):
            at = own_windows + starts[k]
            term_pay_ref[k, group] = rows[at : at + span].astype(jnp.bfloat16)
            term_copy(k, group).start()
        wide_lane = lax.broadcasted_iota(jnp.int32, (windows, LANES), 1)
        weight_sum = jnp.sum(jnp.where(wide_lane >= inner, weight_total, 0.0), axis=1, keepdims=True)
        for c in range(halves):
            local_ref[c, pl.ds(group, windows, stride=GS), :] = rows[:, c * LANES : (c + 1) * LANES]
        local_weight_ref[pl.ds(group, windows, stride=GS), :] = jnp.broadcast_to(
            weight_sum, (windows, LANES)
        )

    @pl.when(step == groups - 1)
    def _():
        for k in range(4):
            start = owned + k * shared
            weight_pay_ref[0, k] = local_weight_ref[start : start + lanes, :].T[:8]
            weight_copy(0, k).start()

        def subtract(chunk, carry):
            at = pl.ds(pl.multiple_of(chunk * LANES, LANES), LANES)
            for c in range(halves):
                values_ref[c, at, :] = (
                    edge_ref[at, c * LANES : (c + 1) * LANES].astype(jnp.float32)
                    - local_ref[c, at, :]
                )
            own = jnp.broadcast_to(owner_ref[:, at], (LANES, LANES)).T
            pre_weight_ref[at, :] = own + local_weight_ref[at, :]
            return carry

        lax.fori_loop(0, owned // LANES, subtract, 0, unroll=6)

        for pair in ((0, 1), (2, 3)):

            def pick(s, carry):
                loaded = []
                for k in pair:
                    r = readers_ref[k, s]
                    loaded.append(
                        (
                            [values_ref[c, pl.ds(r, 1), :] for c in range(halves)],
                            pre_weight_ref[pl.ds(r, 1), :],
                        )
                    )
                for k, (values, weight) in zip(pair, loaded):
                    for c in range(halves):
                        picked_ref[k, c, pl.ds(s, 1), :] = values[c]
                    picked_weight_ref[k, pl.ds(s, 1), :] = weight
                return carry

            lax.fori_loop(0, shared, pick, 0, unroll=12)
            for k in pair:
                for c in range(halves):
                    pick_pay_ref[k, :, c * LANES : (c + 1) * LANES] = picked_ref[k, c].astype(
                        jnp.bfloat16
                    )
                pick_copy(k).start()
                weight_pay_ref[1, k] = picked_weight_ref[k].T[:8]
                weight_copy(1, k).start()

        for k in range(4):

            def settle(g, carry):
                term_copy(k, g).wait()
                return carry

            lax.fori_loop(0, groups, settle, 0)
            weight_copy(0, k).wait()
        for k in range(4):
            for g in range(groups):
                piece = term_got_ref[k, g].astype(jnp.float32)
                for c in range(halves):
                    incoming_ref[k, c, pl.ds(g, span, stride=GS), :] = piece[
                        :, c * LANES : (c + 1) * LANES
                    ]
            shift = shifts[OPPOSITE[k]]
            before = picked_weight_ref[k, :pad, :]
            after = 1.0 / (before + weight_got_ref[0, k].T[:pad, 0:1])
            before = 1.0 / before
            real = lax.broadcasted_iota(jnp.int32, (pad, LANES), 0) < shared
            for c in range(halves):
                picked = picked_ref[k, c]
                incoming = incoming_ref[k, c, shift : shift + pad, :]
                change = (picked - incoming) * after - picked * before
                added_ref[k * lanes : k * lanes + pad, c * LANES : (c + 1) * LANES] = jnp.where(
                    real, change, 0.0
                ).astype(jnp.bfloat16)

        row_ids = lax.broadcasted_iota(jnp.int32, (2 * LANES, 4 * lanes), 0).astype(jnp.int16)
        one, zero = jnp.bfloat16(1), jnp.bfloat16(0)

        def finish(chunk, carry):
            at = pl.ds(pl.multiple_of(chunk * 2 * LANES, 2 * LANES), 2 * LANES)
            wanted = (reader_lane_ref[:1, :] - chunk * 2 * LANES).astype(jnp.int16)
            onehot = jnp.where(row_ids == wanted, one, zero)
            added = jnp.dot(onehot, added_ref[...], preferred_element_type=jnp.float32)
            scale = 1.0 / pre_weight_ref[at, :]
            for c in range(halves):
                values_ref[c, at, :] = (
                    values_ref[c, at, :] * scale + added[:, c * LANES : (c + 1) * LANES]
                )
            return carry

        lax.fori_loop(0, owned // (2 * LANES), finish, 0, unroll=3)
        for c in range(halves):
            face_copy(c).start()

    @pl.when(step == groups)
    def _():
        for k in (2, 3, 0, 1):
            pick_copy(k).wait()
            weight_copy(1, k).wait()
        theirs_ref[...] = jnp.zeros_like(theirs_ref)
        for k in range(4):
            weights = weight_got_ref[1, k].T
            start = owned + k * shared
            scale = 1.0 / (local_weight_ref[start : start + pad, :] + weights[:pad, 0:1])
            for c in range(halves):
                theirs = (
                    pick_got_ref[k, :, c * LANES : (c + 1) * LANES].astype(jnp.float32)
                    - local_ref[c, start : start + pad, :]
                ) * scale
                theirs_ref[c, k * shared : (k + 1) * shared, :] = theirs[:shared]

    @pl.when(step >= groups)
    def _():
        table = jnp.concatenate(
            [
                jnp.concatenate(
                    [
                        values_ref[c, pl.ds(group, own_windows, stride=GS), :],
                        theirs_ref[c, pl.ds(group, windows - own_windows, stride=GS), :],
                    ],
                    axis=0,
                )
                for c in range(halves)
            ],
            axis=1,
        )
        pulled = jnp.dot(
            table.T.astype(jnp.bfloat16), spread_ref[group], preferred_element_type=jnp.float32
        )
        for e in range(GS):
            slot = group * GS + e
            part = pulled[:, e * LANES : (e + 1) * LANES].T[:inner]
            reduced = (load_all_ref[slot].astype(jnp.float32) - part).astype(jnp.bfloat16)
            result = jnp.dot(
                inverse_all_ref[slot], reduced, preferred_element_type=jnp.float32
            )
            result = jnp.where(slot < count_ref[0, 0], result, 0.0)
            for c in range(halves):
                out_rows_ref[c, pl.ds(e, inner, stride=GS), :] = result[
                    :, c * LANES : (c + 1) * LANES
                ]
        out_ref[...] = (
            jnp.concatenate([out_rows_ref[c] for c in range(halves)], axis=1)
            .reshape(inner, GS, columns)
            .astype(jnp.bfloat16)
        )

    @pl.when(step == 2 * groups - 1)
    def _():
        for c in range(halves):
            face_copy(c).wait()


def per_device(
    counts,
    coupling,
    interior_inverse,
    interior_load,
    boundary_load,
    owner_weight,
    elem_weight,
    elem_dof,
    reader_rows,
    elem_count,
):
    slots, modes, inner = coupling.shape[2:]
    columns = interior_load.shape[-1]
    owned = boundary_load.shape[2]
    shared = reader_rows.shape[3]
    groups = slots // GS
    halves = columns // LANES
    windows = round_up((owned + 4 * shared) // GS, 16)
    pad = round_up(shared, 16)
    span = round_up(shared // GS + 2, 16)
    lanes = round_up(shared, LANES)
    own_windows = owned // GS
    shared_windows = windows - own_windows
    sizes = (slots, modes, inner, columns, owned, shared, windows, pad, lanes, span)
    f32, bf16 = jnp.float32, jnp.bfloat16
    smem = pl.BlockSpec(memory_space=pltpu.SMEM)
    vmem = pl.BlockSpec(memory_space=pltpu.VMEM)
    anyplace = pl.BlockSpec(memory_space=pl.ANY)

    def at_first(g):
        return jnp.minimum(g, groups - 1)

    def by_group(*tail):
        zeros = (0,) * len(tail)
        return pl.BlockSpec((None, None, GS) + tail, lambda g: (0, 0, at_first(g)) + zeros)

    def by_mode(rows, width):
        return pl.BlockSpec(
            (None, None, rows, GS, width), lambda g: (0, 0, 0, at_first(g), 0)
        )

    def modes_first(array):
        return jnp.swapaxes(array, 2, 3)

    readers = reader_rows[0, 0]
    params = dict(vmem_limit_bytes=VMEM_BYTES, dimension_semantics=("arbitrary",))
    shape = jax.ShapeDtypeStruct
    face, interior = pl.pallas_call(
        functools.partial(condense_kernel, sizes, counts),
        grid=(2 * groups,),
        in_specs=[
            smem,
            smem,
            by_mode(inner, inner),
            by_mode(inner, columns),
            by_mode(modes, inner),
            by_group(modes),
            by_group(modes),
            vmem,
            vmem,
            vmem,
        ],
        out_specs=[
            anyplace,
            pl.BlockSpec(
                (None, None, inner, GS, columns),
                lambda g: (0, 0, 0, jnp.maximum(g - groups, 0), 0),
            ),
        ],
        out_shape=[
            shape((1, 1, owned, columns), f32),
            shape((1, 1, inner, slots, columns), bf16),
        ],
        scratch_shapes=[
            pltpu.VMEM((halves, owned, LANES), f32),
            pltpu.VMEM((groups, windows, GS * LANES), bf16),
            pltpu.VMEM((slots, inner, inner), bf16),
            pltpu.VMEM((slots, inner, columns), bf16),
            pltpu.VMEM((halves, inner * GS, LANES), f32),
            pltpu.VMEM((halves, windows * GS, LANES), f32),
            pltpu.VMEM((windows * GS + LANES, LANES), f32),
            pltpu.VMEM((owned, LANES), f32),
            pltpu.VMEM((GS, LANES, columns), bf16),
            pltpu.VMEM((inner * GS, LANES), f32),
            pltpu.VMEM((halves, inner * GS, LANES), f32),
            pltpu.VMEM((modes * GS, LANES), f32),
            pltpu.VMEM((4, halves, pad, LANES), f32),
            pltpu.VMEM((4, lanes, LANES), f32),
            pltpu.VMEM((4, halves, span * GS, LANES), f32),
            pltpu.VMEM((4 * lanes, columns), bf16),
            pltpu.VMEM((8, 4 * lanes), jnp.int32),
            pltpu.VMEM((halves, shared_windows * GS, LANES), f32),
            pltpu.VMEM((4, groups, span, columns), bf16),
            pltpu.VMEM((4, groups, span, columns), bf16),
            pltpu.VMEM((4, pad, columns), bf16),
            pltpu.VMEM((4, pad, columns), bf16),
            pltpu.VMEM((2, 4, 8, lanes), f32),
            pltpu.VMEM((2, 4, 8, lanes), f32),
            pltpu.SemaphoreType.DMA((4, groups)),
            pltpu.SemaphoreType.DMA((4, groups)),
            pltpu.SemaphoreType.DMA((3, 4)),
            pltpu.SemaphoreType.DMA((3, 4)),
            pltpu.SemaphoreType.DMA((halves,)),
        ],
        compiler_params=pltpu.CompilerParams(
            collective_id=0, has_side_effects=True, **params
        ),
        name="condense_recover",
    )(
        elem_count,
        readers,
        modes_first(interior_inverse),
        modes_first(interior_load),
        modes_first(coupling),
        elem_weight,
        elem_dof,
        boundary_load[0, 0],
        owner_weight[0],
        readers,
    )
    return face, modes_first(interior)


def solution(mesh):
    in_specs = (
        P("px", "py", None, None, None),
        P("px", "py", None, None, None),
        P("px", "py", None, None, None),
        P("px", "py", None, None),
        P("px", "py", None),
        P("px", "py", None, None),
        P("px", "py", None, None),
        P("px", "py", None, None),
        P("px", "py"),
    )
    out_specs = (P("px", "py", None, None), P("px", "py", None, None, None))
    counts = (mesh.shape["px"], mesh.shape["py"])
    return jax.shard_map(
        functools.partial(per_device, counts),
        mesh=mesh,
        in_specs=in_specs,
        out_specs=out_specs,
        check_vma=False,
    )
```
